512 devices in a mesh: expert: 32 (over z_lo, y), dp: 8 (over x, core), half: 2 (over z_hi).
Axes of the slice: x: 4, y: 8, z: 8 (z_hi: 2, z_lo: 4; z = z_hi * 4 + z_lo), core: 2. Of those that a mesh axis runs over, the one named last changes fastest.
Arguments:
- patches: bfloat16 [65536, 1664], P(('expert', 'dp', 'half')), may hold values from -6 to 6
- upstream: bfloat16 [65536, 1664], P(('expert', 'dp', 'half')), may hold values from -6 to 6
- gates: bfloat16 [65536, 2], P(('expert', 'dp', 'half')), may hold values from 0.099609375 to 0.59765625
- expert_ids: int32 [65536, 2], P(('expert', 'dp', 'half')), may hold values from 0 to 31, as said below
- slot_ids: int32 [65536, 2], P(('expert', 'dp', 'half')), may hold values from -1 to 1, as said below
- in_weights: bfloat16 [32, 3328, 1664], P('expert', ('dp', 'half')), may hold values from -0.15625 to 0.15625
- out_weights: bfloat16 [32, 3328, 1664], P('expert', ('dp', 'half')), may hold values from -0.109375 to 0.109375
Outputs:
- patch_grad: bfloat16 [65536, 1664], P(('expert', 'dp', 'half'))
- gate_grad: float32 [65536, 2], P(('expert', 'dp', 'half'))
- in_weight_grad: bfloat16 [32, 3328, 1664], P('expert', ('dp', 'half'))
- out_weight_grad: bfloat16 [32, 3328, 1664], P('expert', ('dp', 'half'))
The draws below stay inside these ranges and needn't reach their ends.
Inputs may be any that keep to these rules, and one draw needn't show every extreme that they name: `expert_ids`: the two experts of a patch differ; within the 128 patches of one device every expert is named 2 or more times. `slot_ids`: -1 marks a dropped assignment. Within the patches of one device, each expert's slots 0 to 1 are each held by exactly one assignment naming that expert.
All inputs are finite; a program needn't handle non-finite values.
Results may differ from the reference program's by a relative error of at most 0.024.
Values may be sent and summed in bfloat16 or wider, within the bound.
No kernel may reach another device: no remote copies, remote signals or barrier semaphores. Data moves between devices by JAX's collectives and lax.ppermute only.
A program may use at most 64 MiB of HBM per device.

```python
import jax
import jax.numpy as jnp
from jax import lax

D = 1664
H = 3328
T_DEV = 128
CAP = 2
EXPERTS = 32
HS = 208
TOKENS = 65536
N_DP = 8
N_HALF = 2


def shuffled(key, nblock):
    return jax.vmap(lambda single: jax.random.permutation(single, T_DEV))(jax.random.split(key, nblock)).astype(jnp.int32)


def routing(key):
    nblock = TOKENS // T_DEV
    streams = jax.random.split(key, 6)
    placing = shuffled(streams[0], nblock)
    position = jnp.argsort(placing, axis=1).astype(jnp.int32)
    lower = jax.random.randint(streams[1], (nblock, T_DEV), 0, EXPERTS)
    upper = jax.random.randint(streams[2], (nblock, T_DEV), 0, EXPERTS)
    moving = jax.random.randint(streams[3], (nblock, 1), 0, EXPERTS)
    favored = (jnp.minimum(lower, upper) + moving) % EXPERTS
    offset = jax.random.randint(streams[4], (nblock, T_DEV), 1, EXPERTS)
    balanced = position < EXPERTS * CAP
    second = jnp.where(balanced, position % EXPERTS, (favored + offset) % EXPERTS)
    first = jnp.where(balanced, (second + offset) % EXPERTS, favored)
    ordering = shuffled(streams[5], nblock)
    standing = jnp.argsort(ordering, axis=1).astype(jnp.int32)
    sequence = jnp.concatenate([jnp.take_along_axis(first, ordering, axis=1), jnp.take_along_axis(second, ordering, axis=1)], axis=1)
    onehot = (sequence[..., None] == jnp.arange(EXPERTS, dtype=jnp.int32)).astype(jnp.int32)
    before = jnp.cumsum(onehot, axis=1) - onehot
    ranking = jnp.sum(before * onehot, axis=2)
    slotted = jnp.where(ranking < CAP, ranking, -1)
    slot_first = jnp.take_along_axis(slotted[:, :T_DEV], standing, axis=1)
    slot_second = jnp.take_along_axis(slotted[:, T_DEV:], standing, axis=1)
    chosen = jnp.stack([first, second], axis=-1).reshape(TOKENS, 2).astype(jnp.int32)
    placed = jnp.stack([slot_first, slot_second], axis=-1).reshape(TOKENS, 2).astype(jnp.int32)
    return (chosen, placed)


def draw_expert_ids(key, part):
    return routing(key)[0]


def draw_slot_ids(key, part):
    return routing(key)[1]


def steps_of(stream_key, extent, cuts, least, largest):
    level, own = 1.0, jax.random.fold_in(stream_key, 6)
    for dim, blocks in cuts:
        draws = jnp.exp(jax.random.uniform(jax.random.fold_in(own, dim), (blocks,), jnp.float32, least / len(cuts), largest / len(cuts)))
        level = level * jnp.repeat(draws, extent[dim] // blocks).reshape([-1 if axis == dim else 1 for axis in range(len(extent))])
    return level


def gaussian(rng, dims, scale, most, shards=(), kind=jnp.bfloat16):
    result = scale * jax.random.normal(rng, dims, jnp.float32)
    if shards:
        result = result * steps_of(rng, dims, shards, -0.22, 0.18)
    return jnp.clip(result, -most, most).astype(kind)


def setup_inputs(seed: int = 0) -> dict:
    key_of = jax.random.split(jax.random.key(seed), 8)
    return {
        "patches": gaussian(key_of[0], (TOKENS, D), 1.0, 6.0, ((0, 512),)),
        "upstream": gaussian(key_of[1], (TOKENS, D), 1.0, 6.0, ((0, 512),)),
        "gates": jnp.clip(0.099609375 + 0.49804688 * jax.random.uniform(key_of[2], (TOKENS, 2), jnp.float32) ** steps_of(key_of[2], (TOKENS, 2), ((0, 512),), -0.2, 0.2), 0.099609375, 0.59765625).astype(jnp.bfloat16),
        "expert_ids": draw_expert_ids(jax.random.fold_in(key_of[7], 71), 0),
        "slot_ids": draw_slot_ids(jax.random.fold_in(key_of[7], 71), 0),
        "in_weights": gaussian(key_of[5], (EXPERTS, H, D), D ** -0.5, 0.15625, ((0, 32), (1, 16))),
        "out_weights": gaussian(key_of[6], (EXPERTS, H, D), H ** -0.5, 0.109375, ((0, 32), (1, 16))),
    }


ROOT_TERM = 0.7978845608028654
CUBIC_TERM = 0.044715


def gelu_tanh(value):
    inner = ROOT_TERM * (value + CUBIC_TERM * value * value * value)
    return 0.5 * value * (1.0 + jnp.tanh(inner))


def gelu_slope(value):
    inner = ROOT_TERM * (value + CUBIC_TERM * value * value * value)
    tangent = jnp.tanh(inner)
    return 0.5 * (1.0 + tangent) + 0.5 * value * (1.0 - tangent * tangent) * ROOT_TERM * (1.0 + 3.0 * CUBIC_TERM * value * value)


def expert_backward(operands):
    rows_in, rows_up, rows_gate, weight_in, weight_out = operands
    groups = N_DP * N_HALF
    count = rows_in.shape[0]
    preact = jnp.dot(rows_in, weight_in.T, preferred_element_type=jnp.float32)
    hidden_act = gelu_tanh(preact)
    hidden_bf = hidden_act.astype(jnp.bfloat16)
    back_proj = jnp.dot(rows_up, weight_out.T, preferred_element_type=jnp.float32)
    gate_part = jnp.sum((hidden_act * back_proj).reshape(count, groups, HS), axis=2).astype(jnp.bfloat16)
    gate_slot = jnp.sum(gate_part.astype(jnp.float32), axis=1).astype(jnp.bfloat16)
    scale = rows_gate.astype(jnp.float32)[:, None]
    preact_grad = (scale * back_proj * gelu_slope(preact)).astype(jnp.bfloat16)
    scaled_up = (scale * rows_up.astype(jnp.float32)).astype(jnp.bfloat16)
    grad_out = jnp.dot(hidden_bf.T, scaled_up, preferred_element_type=jnp.float32).astype(jnp.bfloat16)
    grad_in = jnp.dot(preact_grad.T, rows_in, preferred_element_type=jnp.float32).astype(jnp.bfloat16)
    input_part = jnp.einsum(
        "rgh,ghd->rgd",
        preact_grad.reshape(count, groups, HS).astype(jnp.float32),
        weight_in.reshape(groups, HS, D).astype(jnp.float32),
    ).astype(jnp.bfloat16)
    patch_slot = jnp.sum(input_part.astype(jnp.float32), axis=1).astype(jnp.bfloat16)
    return patch_slot, gate_slot, grad_in, grad_out


def reference(patches, upstream, gates, expert_ids, slot_ids, in_weights, out_weights):
    nblock = TOKENS // T_DEV
    width = EXPERTS * CAP
    target = jnp.where(slot_ids >= 0, expert_ids * CAP + slot_ids, -1).astype(jnp.int32).reshape(nblock, T_DEV, 2)
    match = target[..., None] == jnp.arange(width, dtype=jnp.int32)
    struck = jnp.any(match, axis=2)
    places = jnp.sum(jnp.where(struck, jnp.arange(T_DEV, dtype=jnp.int32)[None, :, None], 0), axis=1).astype(jnp.int32)
    slot_in = jnp.take_along_axis(patches.reshape(nblock, T_DEV, D), places[..., None], axis=1)
    slot_up = jnp.take_along_axis(upstream.reshape(nblock, T_DEV, D), places[..., None], axis=1)
    gate_blocks = gates.reshape(nblock, T_DEV, 2).astype(jnp.float32)[..., None]
    slot_gate = jnp.sum(jnp.where(match, gate_blocks, 0.0), axis=(1, 2)).astype(jnp.bfloat16)

    def by_expert(array):
        shaped = array.reshape((nblock, EXPERTS, CAP) + array.shape[2:])
        return jnp.moveaxis(shaped, 1, 0).reshape((EXPERTS, nblock * CAP) + array.shape[2:])

    patch_slot, gate_slot, grad_in, grad_out = lax.map(
        expert_backward,
        (by_expert(slot_in), by_expert(slot_up), by_expert(slot_gate), in_weights, out_weights),
    )
    patch_back = jnp.moveaxis(patch_slot.reshape(EXPERTS, nblock, CAP, D), 0, 1).reshape(nblock, width, D)
    gate_back = jnp.moveaxis(gate_slot.reshape(EXPERTS, nblock, CAP), 0, 1).reshape(nblock, width)
    valid = target >= 0
    index = jnp.maximum(target, 0).reshape(nblock, T_DEV * 2).astype(jnp.int32)
    picked = jnp.take_along_axis(patch_back, index[..., None], axis=1).reshape(nblock, T_DEV, 2, D)
    patch_grad = jnp.sum(jnp.where(valid[..., None], picked.astype(jnp.float32), 0.0), axis=2)
    patch_grad = patch_grad.astype(jnp.bfloat16).reshape(TOKENS, D)
    picked_gate = jnp.take_along_axis(gate_back, index, axis=1).reshape(nblock, T_DEV, 2)
    gate_grad = jnp.where(valid, picked_gate.astype(jnp.float32), 0.0).reshape(TOKENS, 2)
    return patch_grad, gate_grad, grad_in, grad_out
```

```python
import jax
import jax.numpy as jnp
from jax import lax
from jax.experimental import pallas as pl
from jax.experimental.pallas import tpu as pltpu
from jax.sharding import Mesh, PartitionSpec as P

F32 = jnp.float32
BF16 = jnp.bfloat16
I32 = jnp.int32

CAP = 2
ROOT_TERM = 0.7978845608028654
CUBIC_TERM = 0.044715

T = 128
D = 1664
HS = 208
X = 4
SRC = 64
ROWS = SRC * CAP
SEND = SRC * 8
HALF_W = 896
QW = 512
GW = D + 128
VMEM_LIMIT = 56 * 1024 * 1024


def params():
    return pltpu.CompilerParams(vmem_limit_bytes=VMEM_LIMIT)


def dot(left, right):
    return jnp.dot(left, right, preferred_element_type=F32)


def dot_rows(left, right):
    return lax.dot_general(left, right, (((0,), (0,)), ((), ())), preferred_element_type=F32)


def dot_width(left, right):
    return lax.dot_general(left, right, (((1,), (1,)), ((), ())), preferred_element_type=F32)


def slot_match(ids, slots):
    target = jnp.where(slots >= 0, ids * CAP + slots, -1)
    row = lax.broadcasted_iota(I32, (T, SEND), 1)
    slot = (row >> 4) * CAP + (row & 1)
    return target[:, 0:1] == slot, target[:, 1:2] == slot, row


def pack_rows_kernel(patches, upstream, gates, ids, slots, out):
    m0, m1, row = slot_match(ids[...], slots[...])
    g = gates[...].astype(F32)
    hit = jnp.where(m0 | m1, 1.0, 0.0)
    gate = jnp.where(m0, g[:, 0:1], 0.0) + jnp.where(m1, g[:, 1:2], 0.0)
    is_up = (row & 2) != 0
    right = (row & 4) != 0
    p_sel = jnp.where(is_up, 0.0, hit)
    u_sel = jnp.where(is_up, gate, 0.0)
    p_l = jnp.where(right, 0.0, p_sel).astype(BF16)
    p_r = jnp.where(right, p_sel, 0.0).astype(BF16)
    u_l = jnp.where(right, 0.0, u_sel).astype(BF16)
    u_r = jnp.where(right, u_sel, 0.0).astype(BF16)
    rest = D - HALF_W
    out[:, :rest] = (
        dot_rows(p_l, patches[:, :rest])
        + dot_rows(u_l, upstream[:, :rest])
        + dot_rows(p_r, patches[:, HALF_W:])
        + dot_rows(u_r, upstream[:, HALF_W:])
    ).astype(BF16)
    out[:, rest:] = (
        dot_rows(p_l, patches[:, rest:HALF_W]) + dot_rows(u_l, upstream[:, rest:HALF_W])
    ).astype(BF16)


def unpack_rows_kernel(got, out):
    part = 256
    o = lax.broadcasted_iota(I32, (128, part), 0)
    c = lax.broadcasted_iota(I32, (128, part), 1)
    want = ((o & 63) >> 1) * 8 + (o >> 6) * 2 + (o & 1)
    for g in range(SEND // part):
        block = got[pl.ds(g * part, part), :]
        for h in range(2):
            sel = jnp.where(c == want + 4 * h, 1.0, 0.0).astype(BF16)
            wide = HALF_W if h == 0 else D - HALF_W
            rows = dot(sel, block[:, :wide]).astype(BF16)
            out[pl.ds(g * 64, 64), pl.ds(h * HALF_W, wide)] = rows[:64]
            out[pl.ds(ROWS + g * 64, 64), pl.ds(h * HALF_W, wide)] = rows[64:]


def gelu_and_slope(value):
    square = value * value
    tangent = jnp.tanh(ROOT_TERM * value * (1.0 + CUBIC_TERM * square))
    up = 0.5 * (1.0 + tangent)
    slope = up + 0.5 * value * (1.0 - tangent * tangent) * ROOT_TERM * (1.0 + 3.0 * CUBIC_TERM * square)
    return value * up, slope


def load_rows(sources, p_all, u_all, sems):
    copies = []
    for b, source in enumerate(sources):
        for k, place in enumerate((p_all, u_all)):
            copy = pltpu.make_async_copy(
                source.at[pl.ds(k * ROWS, ROWS), :], place.at[pl.ds(b * ROWS, ROWS), :], sems.at[k, b]
            )
            copy.start()
            copies.append(copy)
    for copy in copies:
        copy.wait()


def expert_kernel(r0, r1, r2, r3, wi0, wi1, wo0, wo1, i0, i1, i2, i3, pg_out, hid_out, p_all, u_all, sems):
    load_rows((r0, r1, r2, r3), p_all, u_all, sems)
    gate = jnp.zeros((X * ROWS, 1), F32)
    grads = []
    for c, (wi, wo) in enumerate(((wi0, wo0), (wi1, wo1))):
        pre = dot_width(p_all[...], wi[...])
        back = dot_width(u_all[...], wo[...])
        hid, slope = gelu_and_slope(pre)
        gate += jnp.sum(hid * back, axis=1, keepdims=True)
        pg = (back * slope).astype(BF16)
        pg_out[c] = pg
        hid_out[c] = hid.astype(BF16)
        grads.append(pg)
    lane = lax.broadcasted_iota(I32, (ROWS, 128), 1)
    for b, out in enumerate((i0, i1, i2, i3)):
        rows = slice(b * ROWS, (b + 1) * ROWS)
        out[:, :D] = (dot(grads[0][rows], wi0[...]) + dot(grads[1][rows], wi1[...])).astype(BF16)
        out[:, D:] = jnp.where(lane == 0, gate[rows], 0.0).astype(BF16)


def weight_kernel(r0, r1, r2, r3, pg, hid, own_in, own_out, other, p_all, u_all, sems):
    load_rows((r0, r1, r2, r3), p_all, u_all, sems)
    own_in[...] = dot_rows(pg[0], p_all[...])
    own_out[...] = dot_rows(hid[0], u_all[...])
    other[pl.ds(0, HS), :] = dot_rows(pg[1], p_all[...]).astype(BF16)
    other[pl.ds(HS, HS), :] = dot_rows(hid[1], u_all[...]).astype(BF16)


def weight_sum_kernel(own_in, own_out, got, grad_in, grad_out):
    grad_in[...] = (own_in[...] + got[pl.ds(0, HS), :].astype(F32)).astype(BF16)
    grad_out[...] = (own_out[...] + got[pl.ds(HS, HS), :].astype(F32)).astype(BF16)


def pack_back_kernel(i0, i1, i2, i3, out):
    total = (
        (i0[...].astype(F32) + i1[...].astype(F32)) + (i2[...].astype(F32) + i3[...].astype(F32))
    ).astype(BF16)
    row = lax.broadcasted_iota(I32, (SEND, ROWS), 0)
    col = lax.broadcasted_iota(I32, (SEND, ROWS), 1)
    want = (row >> 3) * 2 + (row & 1)
    quarter = (row >> 1) & 3
    sels = [jnp.where((col == want) & (quarter == q), 1.0, 0.0).astype(BF16) for q in range(4)]
    last = GW - 3 * QW
    narrow = sum(dot(sels[q], total[:, q * QW : q * QW + last]) for q in range(4))
    wide = sum(dot(sels[q], total[:, q * QW + last : (q + 1) * QW]) for q in range(3))
    out[:, :last] = narrow.astype(BF16)
    out[:, last:] = wide.astype(BF16)


def unpack_back_kernel(got, gates, ids, slots, patch_grad, gate_grad):
    m0, m1, row = slot_match(ids[...], slots[...])
    quarter = (row >> 1) & 3
    hit = jnp.where(m0 | m1, 1.0, 0.0)
    for q in range(4):
        wide = QW if q < 3 else D - 3 * QW
        sel = jnp.where(quarter == q, hit, 0.0).astype(BF16)
        patch_grad[:, pl.ds(q * QW, wide)] = dot(sel, got[:, :wide]).astype(BF16)
    gate_block = got[:, D - 3 * QW : GW - 3 * QW]
    g = gates[...].astype(F32)
    for k, m in enumerate((m0, m1)):
        sel = jnp.where((quarter == 3) & m, 1.0, 0.0).astype(BF16)
        gate_grad[:, k : k + 1] = dot(sel, gate_block)[:, 0:1] / g[:, k : k + 1]


def shape(dims, kind=BF16):
    return jax.ShapeDtypeStruct(dims, kind)


ANY = pl.BlockSpec(memory_space=pl.ANY)
VM = pl.BlockSpec(memory_space=pltpu.VMEM)


def call(kernel, out_shape, args, flops, moved, in_specs=None, scratch=()):
    return pl.pallas_call(
        kernel,
        out_shape=out_shape,
        in_specs=in_specs or [VM] * len(args),
        out_specs=jax.tree.map(lambda _: VM, out_shape),
        scratch_shapes=scratch,
        compiler_params=params(),
        cost_estimate=pl.CostEstimate(flops=flops, bytes_accessed=moved, transcendentals=0),
    )(*args)


def shift(value, axis, by):
    size = lax.axis_size(axis)
    return lax.ppermute(value, axis, [(i, (i + by) % size) for i in range(size)])


def local(patches, upstream, gates, ids, slots, in_weights, out_weights):
    everywhere = ("zlo", "y", "zhi")
    wi, wo = in_weights[0], out_weights[0]
    sent = call(
        pack_rows_kernel, shape((SEND, HALF_W)), (patches, upstream, gates, ids, slots), 500_000_000, 2_000_000
    )
    got = lax.all_to_all(sent, everywhere, split_axis=0, concat_axis=0, tiled=True)
    own = call(unpack_rows_kernel, shape((2 * ROWS, D)), (got,), 300_000_000, 2_000_000)
    blocks = [own] + [shift(own, "x", by) for by in (1, 2, 3)]
    wi1, wo1 = shift(wi, "core", 1), shift(wo, "core", 1)
    scratch = (
        pltpu.VMEM((X * ROWS, D), BF16),
        pltpu.VMEM((X * ROWS, D), BF16),
        pltpu.SemaphoreType.DMA((2, X)),
    )
    hidden = shape((2, X * ROWS, HS))
    *parts, pg, hid = call(
        expert_kernel,
        [shape((ROWS, GW))] * X + [hidden, hidden],
        (*blocks, wi, wi1, wo, wo1),
        2_200_000_000,
        9_000_000,
        in_specs=[ANY] * X + [VM] * 4,
        scratch=scratch,
    )
    returned = [parts[0]] + [shift(parts[by], "x", X - by) for by in (1, 2, 3)]
    own_in, own_out, other = call(
        weight_kernel,
        [shape((HS, D), F32), shape((HS, D), F32), shape((2 * HS, D))],
        (*blocks, pg, hid),
        1_400_000_000,
        9_000_000,
        in_specs=[ANY] * X + [VM] * 2,
        scratch=scratch,
    )
    other = shift(other, "core", 1)
    grad_in, grad_out = call(
        weight_sum_kernel, [shape((HS, D)), shape((HS, D))], (own_in, own_out, other), 1_000_000, 6_000_000
    )
    back = call(pack_back_kernel, shape((SEND, QW)), returned, 300_000_000, 2_500_000)
    back = lax.all_to_all(back, everywhere, split_axis=0, concat_axis=0, tiled=True)
    patch_grad, gate_grad = call(
        unpack_back_kernel,
        [shape((T, D)), shape((T, 2), F32)],
        (back, gates, ids, slots),
        300_000_000,
        1_000_000,
    )
    return patch_grad, gate_grad, grad_in[None], grad_out[None]


def solution(mesh):
    names = ("zlo", "y", "x", "core", "zhi")
    split = Mesh(mesh.devices.reshape(4, 8, 4, 2, 2), names)
    tokens = P(names, None)
    weights = P(("zlo", "y"), ("x", "core", "zhi"), None)
    return jax.shard_map(
        local,
        mesh=split,
        in_specs=(tokens,) * 5 + (weights,) * 2,
        out_specs=(tokens, tokens, weights, weights),
        check_vma=False,
    )
```

```python
import functools

import jax
import jax.numpy as jnp
from jax import lax
from jax.experimental import pallas as pl
from jax.experimental.pallas import tpu as pltpu
from jax.sharding import Mesh, PartitionSpec as P

F32 = jnp.float32
BF16 = jnp.bfloat16
I32 = jnp.int32

CAP = 2
ROOT_TERM = 0.7978845608028654
CUBIC_TERM = 0.044715

T = 128
D = 1664
HS = 208
SRC = 64
ROWS = SRC * CAP
SEND = SRC * 8
HALF_W = 896
QW = 512
GW = D + 128


def dot(left, right):
    return jnp.dot(left, right, preferred_element_type=F32)


def dot_rows(left, right):
    return lax.dot_general(left, right, (((0,), (0,)), ((), ())), preferred_element_type=F32)


def dot_width(left, right):
    return lax.dot_general(left, right, (((1,), (1,)), ((), ())), preferred_element_type=F32)


def slot_match(ids, slots):
    target = jnp.where(slots >= 0, ids * CAP + slots, -1)
    row = lax.broadcasted_iota(I32, (SEND, T), 0)
    slot = (row >> 4) * CAP + (row & 1)
    return target[0:1, :] == slot, target[1:2, :] == slot, row


def pack_rows_kernel(patches, upstream, gates, ids, slots, w_in, w_out, out, w_both, sems):
    copies = [
        pltpu.make_async_copy(w, w_both.at[pl.ds(k * HS, HS), :], sems.at[k]) for k, w in enumerate((w_in, w_out))
    ]
    for copy in copies:
        copy.start()
    m0, m1, row = slot_match(ids[...], slots[...])
    g = gates[...].astype(F32)
    hit = jnp.where(m0 | m1, 1.0, 0.0)
    gate = jnp.where(m0, g[0:1, :], 0.0) + jnp.where(m1, g[1:2, :], 0.0)
    is_up = (row & 2) != 0
    right = (row & 4) != 0
    p_sel = jnp.where(is_up, 0.0, hit)
    u_sel = jnp.where(is_up, gate, 0.0)
    p_l = jnp.where(right, 0.0, p_sel).astype(BF16)
    p_r = jnp.where(right, p_sel, 0.0).astype(BF16)
    u_l = jnp.where(right, 0.0, u_sel).astype(BF16)
    u_r = jnp.where(right, u_sel, 0.0).astype(BF16)
    rest = D - HALF_W
    out[:, :rest] = (
        dot(p_l, patches[:, :rest])
        + dot(u_l, upstream[:, :rest])
        + dot(p_r, patches[:, HALF_W:])
        + dot(u_r, upstream[:, HALF_W:])
    ).astype(BF16)
    out[:, rest:] = (dot(p_l, patches[:, rest:HALF_W]) + dot(u_l, upstream[:, rest:HALF_W])).astype(BF16)
    for copy in copies:
        copy.wait()


def unpack_rows_kernel(got, out):
    part = 256
    o = lax.broadcasted_iota(I32, (128, part), 0)
    c = lax.broadcasted_iota(I32, (128, part), 1)
    want = ((o & 63) >> 1) * 8 + (o >> 6) * 2 + (o & 1)
    for g in range(SEND // part):
        block = got[pl.ds(g * part, part), :]
        for h in range(2):
            sel = jnp.where(c == want + 4 * h, 1.0, 0.0).astype(BF16)
            wide = HALF_W if h == 0 else D - HALF_W
            rows = dot(sel, block[:, :wide]).astype(BF16)
            out[pl.ds(g * 64, 64), pl.ds(h * HALF_W, wide)] = rows[:64]
            out[pl.ds(ROWS + g * 64, 64), pl.ds(h * HALF_W, wide)] = rows[64:]


def gelu_and_slope(value):
    square = value * value
    tangent = jnp.tanh(ROOT_TERM * value * (1.0 + CUBIC_TERM * square))
    up = 0.5 * (1.0 + tangent)
    slope = up + 0.5 * value * (1.0 - tangent * tangent) * ROOT_TERM * (1.0 + 3.0 * CUBIC_TERM * square)
    return value * up, slope


def expert_kernel(rows, w0, w1, w2, w3, part, pg_out, hid_out):
    p, u = rows[pl.ds(0, ROWS), :], rows[pl.ds(ROWS, ROWS), :]
    gate = jnp.zeros((ROWS, 1), F32)
    total = jnp.zeros((ROWS, D), F32)
    for c, w in enumerate((w0, w1, w2, w3)):
        pre = dot_width(p, w[pl.ds(0, HS), :])
        back = dot_width(u, w[pl.ds(HS, HS), :])
        hid, slope = gelu_and_slope(pre)
        gate += jnp.sum(hid * back, axis=1, keepdims=True)
        pg = (back * slope).astype(BF16)
        pg_out[c] = pg
        hid_out[c] = hid.astype(BF16)
        total += dot(pg, w[pl.ds(0, HS), :])
    part[:, :D] = total.astype(BF16)
    lane = lax.broadcasted_iota(I32, (ROWS, 128), 1)
    part[:, D:] = jnp.where(lane == 0, gate, 0.0).astype(BF16)


def weight_grads(c, rows0, rows1, pg0, pg1, hid0, hid1):
    p0, u0 = rows0[pl.ds(0, ROWS), :], rows0[pl.ds(ROWS, ROWS), :]
    p1, u1 = rows1[pl.ds(0, ROWS), :], rows1[pl.ds(ROWS, ROWS), :]
    return (
        dot_rows(pg0[c], p0) + dot_rows(pg1[c], p1),
        dot_rows(hid0[c], u0) + dot_rows(hid1[c], u1),
    )


def weight_kernel(c, kind, add, *refs):
    out = refs[-1]
    grad_in, grad_out = weight_grads(c, *refs[:6])
    if add:
        got = refs[6]
        grad_in += got[pl.ds(0, HS), :].astype(F32)
        grad_out += got[pl.ds(HS, HS), :].astype(F32)
    out[pl.ds(0, HS), :] = grad_in.astype(kind)
    out[pl.ds(HS, HS), :] = grad_out.astype(kind)


def weight_sum_kernel(own, got, grad_in, grad_out):
    grad_in[...] = (own[pl.ds(0, HS), :] + got[pl.ds(0, HS), :].astype(F32)).astype(BF16)
    grad_out[...] = (own[pl.ds(HS, HS), :] + got[pl.ds(HS, HS), :].astype(F32)).astype(BF16)


def pack_back_kernel(i0, i1, out):
    total = (i0[...].astype(F32) + i1[...].astype(F32)).astype(BF16)
    row = lax.broadcasted_iota(I32, (SEND, ROWS), 0)
    col = lax.broadcasted_iota(I32, (SEND, ROWS), 1)
    want = (row >> 3) * 2 + (row & 1)
    quarter = (row >> 1) & 3
    sels = [jnp.where((col == want) & (quarter == q), 1.0, 0.0).astype(BF16) for q in range(4)]
    last = GW - 3 * QW
    narrow = sum(dot(sels[q], total[:, q * QW : q * QW + last]) for q in range(4))
    wide = sum(dot(sels[q], total[:, q * QW + last : (q + 1) * QW]) for q in range(3))
    out[:, :last] = narrow.astype(BF16)
    out[:, last:] = wide.astype(BF16)


def unpack_back_kernel(got, gates, ids, slots, patch_grad, gate_grad):
    m0, m1, row = slot_match(ids[...], slots[...])
    quarter = (row >> 1) & 3
    hit = jnp.where(m0 | m1, 1.0, 0.0)
    for q in range(4):
        wide = QW if q < 3 else D - 3 * QW
        sel = jnp.where(quarter == q, hit, 0.0).astype(BF16)
        patch_grad[:, pl.ds(q * QW, wide)] = dot_rows(sel, got[:, :wide]).astype(BF16)
    gate_block = got[:, D - 3 * QW : GW - 3 * QW]
    g = gates[...].astype(F32)
    for k, m in enumerate((m0, m1)):
        sel = jnp.where((quarter == 3) & m, 1.0, 0.0).astype(BF16)
        gate_grad[k : k + 1, :] = dot_rows(gate_block, sel)[0:1, :] / g[k : k + 1, :]


def shape(dims, kind=BF16):
    return jax.ShapeDtypeStruct(dims, kind)


ANY = pl.BlockSpec(memory_space=pl.ANY)
VM = pl.BlockSpec(memory_space=pltpu.VMEM)


def call(kernel, out_shape, args, flops, moved, vmem, in_specs=None, out_specs=None, scratch=()):
    return pl.pallas_call(
        kernel,
        out_shape=out_shape,
        in_specs=in_specs or [VM] * len(args),
        out_specs=out_specs or jax.tree.map(lambda _: VM, out_shape),
        scratch_shapes=scratch,
        compiler_params=pltpu.CompilerParams(vmem_limit_bytes=vmem * 1024 * 1024),
        cost_estimate=pl.CostEstimate(flops=flops, bytes_accessed=moved, transcendentals=0),
    )(*args)


def swap(value, axis, partner):
    return lax.ppermute(value, axis, [(i, partner(i)) for i in range(lax.axis_size(axis))])


def swap_rows(value):
    return swap(value, "x", lambda i: i ^ 1)


def swap_weights(value):
    return swap(value, "x", lambda i: 3 - i)


def swap_core(value):
    return swap(value, "core", lambda i: 1 - i)


def local(patches, upstream, gates, ids, slots, in_weights, out_weights):
    everywhere = ("zlo", "y", "zhi")
    gates, ids, slots = gates.T, ids.T, slots.T
    both = shape((2 * HS, D))
    sent, w00 = call(
        pack_rows_kernel,
        [shape((SEND, HALF_W)), both],
        (patches, upstream, gates, ids, slots, in_weights[0], out_weights[0]),
        500_000_000,
        5_000_000,
        16,
        in_specs=[VM] * 5 + [ANY] * 2,
        out_specs=[VM, ANY],
        scratch=[pltpu.SemaphoreType.DMA((2,))],
    )
    w01 = swap_weights(w00)
    got = lax.all_to_all(sent, everywhere, split_axis=0, concat_axis=0, tiled=True)
    own = call(unpack_rows_kernel, shape((2 * ROWS, D)), (got,), 300_000_000, 2_000_000, 16)
    other = swap_rows(own)
    w10, w11 = swap_core(w00), swap_core(w01)
    hidden = shape((4, ROWS, HS))
    expert_out = [shape((ROWS, GW)), hidden, hidden]
    weights = (w00, w10, w01, w11)
    part_own, pg_own, hid_own = call(expert_kernel, expert_out, (own, *weights), 1_100_000_000, 8_000_000, 24)
    part_other, pg_other, hid_other = call(
        expert_kernel, expert_out, (other, *weights), 1_100_000_000, 8_000_000, 24
    )
    part_back = swap_rows(part_other)
    saved = (own, other, pg_own, pg_other, hid_own, hid_other)

    def weight_call(c, kind, add=()):
        return call(
            functools.partial(weight_kernel, c, kind, len(add)),
            shape((2 * HS, D), kind),
            (*saved, *add),
            700_000_000,
            4_000_000,
            24,
        )

    far = swap_core(weight_call(3, BF16))
    near = swap_core(weight_call(1, BF16))
    far = swap_weights(weight_call(2, BF16, (far,)))
    near = weight_call(0, F32, (near,))
    back = call(pack_back_kernel, shape((SEND, QW)), (part_own, part_back), 300_000_000, 2_500_000, 16)
    back = lax.all_to_all(back, everywhere, split_axis=0, concat_axis=0, tiled=True)
    grad_in, grad_out = call(
        weight_sum_kernel, [shape((HS, D)), shape((HS, D))], (near, far), 1_000_000, 6_000_000, 16
    )
    patch_grad, gate_grad = call(
        unpack_back_kernel,
        [shape((T, D)), shape((2, T), F32)],
        (back, gates, ids, slots),
        300_000_000,
        1_000_000,
        16,
    )
    return patch_grad, gate_grad.T, grad_in[None], grad_out[None]


def solution(mesh):
    names = ("zlo", "y", "x", "core", "zhi")
    split = Mesh(mesh.devices.reshape(4, 8, 4, 2, 2), names)
    tokens = P(names, None)
    weights = P(("zlo", "y"), ("x", "core", "zhi"), None)
    return jax.shard_map(
        local,
        mesh=split,
        in_specs=(tokens,) * 5 + (weights,) * 2,
        out_specs=(tokens, tokens, weights, weights),
        check_vma=False,
    )
```

```python
import functools

import jax
import jax.numpy as jnp
from jax import lax
from jax.experimental import pallas as pl
from jax.experimental.pallas import tpu as pltpu
from jax.sharding import Mesh, PartitionSpec as P

F32 = jnp.float32
BF16 = jnp.bfloat16
I32 = jnp.int32

CAP = 2
ROOT_TERM = 0.7978845608028654
CUBIC_TERM = 0.044715

T = 128
D = 1664
HS = 208
SRC = 64
ROWS = SRC * CAP
SEND = SRC * 8
PAD = 256
HALF_W = 896
QW = 512
GW = D + 128


def dot(left, right):
    return jnp.dot(left, right, preferred_element_type=F32)


def dot_rows(left, right):
    return lax.dot_general(left, right, (((0,), (0,)), ((), ())), preferred_element_type=F32)


def dot_width(left, right):
    return lax.dot_general(left, right, (((1,), (1,)), ((), ())), preferred_element_type=F32)


def slot_match(ids, slots):
    target = jnp.where(slots >= 0, ids * CAP + slots, -1)
    row = lax.broadcasted_iota(I32, (SEND, T), 0)
    slot = (row >> 4) * CAP + (row & 1)
    return target[0:1, :] == slot, target[1:2, :] == slot, row


def start_copies(pairs, sems):
    copies = [pltpu.make_async_copy(source, place, sems.at[k]) for k, (source, place) in enumerate(pairs)]
    for copy in copies:
        copy.start()
    return copies


def pack_rows_kernel(
    gates_in, ids_in, slots_in, patches_in, upstream_in, out,
    gates, ids, slots, patches, upstream, packed, sems, out_sem,
):
    copies = start_copies(
        [
            (gates_in, gates),
            (ids_in, ids),
            (slots_in, slots),
            (patches_in, patches),
            (upstream_in, upstream),
        ],
        sems,
    )
    for copy in copies[:3]:
        copy.wait()
    m0, m1, row = slot_match(ids[...], slots[...])
    g = gates[...].astype(F32)
    hit = jnp.where(m0 | m1, 1.0, 0.0)
    gate = jnp.where(m0, g[0:1, :], 0.0) + jnp.where(m1, g[1:2, :], 0.0)
    is_up = (row & 2) != 0
    right = (row & 4) != 0
    p_sel = jnp.where(is_up, 0.0, hit)
    u_sel = jnp.where(is_up, gate, 0.0)
    p_l = jnp.where(right, 0.0, p_sel).astype(BF16)
    p_r = jnp.where(right, p_sel, 0.0).astype(BF16)
    u_l = jnp.where(right, 0.0, u_sel).astype(BF16)
    u_r = jnp.where(right, u_sel, 0.0).astype(BF16)
    for copy in copies[3:]:
        copy.wait()
    rest = D - HALF_W
    packed[:, :rest] = (
        dot(p_l, patches[:, :rest])
        + dot(u_l, upstream[:, :rest])
        + dot(p_r, patches[:, HALF_W:])
        + dot(u_r, upstream[:, HALF_W:])
    ).astype(BF16)
    packed[:, rest:] = (dot(p_l, patches[:, rest:HALF_W]) + dot(u_l, upstream[:, rest:HALF_W])).astype(BF16)
    done = pltpu.make_async_copy(packed, out, out_sem)
    done.start()
    done.wait()


def unpack_rows_kernel(got_in, out, got, sems):
    part = 256
    copies = start_copies(
        [(got_in.at[pl.ds(g * part, part), :], got.at[pl.ds(g * part, part), :]) for g in range(SEND // part)], sems
    )
    o = lax.broadcasted_iota(I32, (128, part), 0)
    c = lax.broadcasted_iota(I32, (128, part), 1)
    want = ((o & 63) >> 1) * 8 + (o >> 6) * 2 + (o & 1)
    for g in range(SEND // part):
        copies[g].wait()
        block = got[pl.ds(g * part, part), :]
        for h in range(2):
            sel = jnp.where(c == want + 4 * h, 1.0, 0.0).astype(BF16)
            wide = HALF_W if h == 0 else D - HALF_W
            rows = dot(sel, block[:, :wide]).astype(BF16)
            out[pl.ds(g * 64, 64), pl.ds(h * HALF_W, wide)] = rows[:64]
            out[pl.ds(ROWS + g * 64, 64), pl.ds(h * HALF_W, wide)] = rows[64:]


def gelu_and_slope(value):
    square = value * value
    tangent = jnp.tanh(ROOT_TERM * value * (1.0 + CUBIC_TERM * square))
    up = 0.5 * (1.0 + tangent)
    slope = up + 0.5 * value * (1.0 - tangent * tangent) * ROOT_TERM * (1.0 + 3.0 * CUBIC_TERM * square)
    return value * up, slope


def turn_kernel(in0, in1, out0, out1, in_turned, out_turned):
    for turned, parts in ((in_turned, (in0, in1)), (out_turned, (out0, out1))):
        for k, part in enumerate(parts):
            turned[:, pl.ds(k * PAD, HS)] = part[...].T
            turned[:, pl.ds(k * PAD + HS, PAD - HS)] = jnp.zeros((D, PAD - HS), BF16)


def expert_kernel(rows, t_in0, t_in1, t_out0, t_out1, w0, w1, w2, w3, part, pg_out, hid_out):
    p, u = rows[pl.ds(0, ROWS), :], rows[pl.ds(ROWS, ROWS), :]
    gate = jnp.zeros((ROWS, 1), F32)
    grads = []
    for c, (t_in, t_out) in enumerate(((t_in0, t_out0), (t_in1, t_out1))):
        pre = dot(p, t_in[...])
        back = dot(u, t_out[...])
        hid, slope = gelu_and_slope(pre)
        gate += jnp.sum(hid * back, axis=1, keepdims=True)
        pg = (back * slope).astype(BF16)
        hid = hid.astype(BF16)
        for k in range(2):
            own = slice(k * PAD, k * PAD + HS)
            pg_out[2 * c + k] = pg[:, own]
            hid_out[2 * c + k] = hid[:, own]
            grads.append(pg[:, own])
    total = sum(dot(grad, w[...]) for grad, w in zip(grads, (w0, w1, w2, w3)))
    part[:, :D] = total.astype(BF16)
    lane = lax.broadcasted_iota(I32, (ROWS, 128), 1)
    part[:, D:] = jnp.where(lane == 0, gate, 0.0).astype(BF16)


def weight_grads(c, rows0, rows1, pg0, pg1, hid0, hid1):
    p0, u0 = rows0[pl.ds(0, ROWS), :], rows0[pl.ds(ROWS, ROWS), :]
    p1, u1 = rows1[pl.ds(0, ROWS), :], rows1[pl.ds(ROWS, ROWS), :]
    return (
        dot_rows(pg0[c], p0) + dot_rows(pg1[c], p1),
        dot_rows(hid0[c], u0) + dot_rows(hid1[c], u1),
    )


def weight_kernel(c, add, *refs):
    out = refs[-1]
    grad_in, grad_out = weight_grads(c, *refs[:6])
    if add:
        got = refs[6]
        grad_in += got[pl.ds(0, HS), :].astype(F32)
        grad_out += got[pl.ds(HS, HS), :].astype(F32)
    out[pl.ds(0, HS), :] = grad_in.astype(BF16)
    out[pl.ds(HS, HS), :] = grad_out.astype(BF16)


def last_weight_kernel(*refs):
    near, far, out_in, out_out = refs[6:]
    grad_in, grad_out = weight_grads(0, *refs[:6])
    top, low = pl.ds(0, HS), pl.ds(HS, HS)
    out_in[...] = (grad_in + near[top, :].astype(F32) + far[top, :].astype(F32)).astype(BF16)
    out_out[...] = (grad_out + near[low, :].astype(F32) + far[low, :].astype(F32)).astype(BF16)


def pack_back_kernel(i0, i1, out):
    total = (i0[...].astype(F32) + i1[...].astype(F32)).astype(BF16)
    row = lax.broadcasted_iota(I32, (SEND, ROWS), 0)
    col = lax.broadcasted_iota(I32, (SEND, ROWS), 1)
    want = (row >> 3) * 2 + (row & 1)
    quarter = (row >> 1) & 3
    sels = [jnp.where((col == want) & (quarter == q), 1.0, 0.0).astype(BF16) for q in range(4)]
    last = GW - 3 * QW
    narrow = sum(dot(sels[q], total[:, q * QW : q * QW + last]) for q in range(4))
    wide = sum(dot(sels[q], total[:, q * QW + last : (q + 1) * QW]) for q in range(3))
    out[:, :last] = narrow.astype(BF16)
    out[:, last:] = wide.astype(BF16)


def unpack_back_kernel(got, gates, ids, slots, patch_grad, gate_grad):
    m0, m1, row = slot_match(ids[...], slots[...])
    quarter = (row >> 1) & 3
    hit = jnp.where(m0 | m1, 1.0, 0.0)
    for q in range(4):
        wide = QW if q < 3 else D - 3 * QW
        sel = jnp.where(quarter == q, hit, 0.0).astype(BF16)
        patch_grad[:, pl.ds(q * QW, wide)] = dot_rows(sel, got[:, :wide]).astype(BF16)
    gate_block = got[:, D - 3 * QW : GW - 3 * QW]
    g = gates[...].astype(F32)
    for k, m in enumerate((m0, m1)):
        sel = jnp.where((quarter == 3) & m, 1.0, 0.0).astype(BF16)
        gate_grad[k : k + 1, :] = dot_rows(gate_block, sel)[0:1, :] / g[k : k + 1, :]


def shape(dims, kind=BF16):
    return jax.ShapeDtypeStruct(dims, kind)


ANY = pl.BlockSpec(memory_space=pl.ANY)
HBM = pl.BlockSpec(memory_space=pltpu.HBM)
VM = pl.BlockSpec(memory_space=pltpu.VMEM)


def call(kernel, out_shape, args, flops, moved, vmem, in_specs=None, out_specs=None, scratch=()):
    return pl.pallas_call(
        kernel,
        out_shape=out_shape,
        in_specs=in_specs or [VM] * len(args),
        out_specs=out_specs or jax.tree.map(lambda _: VM, out_shape),
        scratch_shapes=scratch,
        compiler_params=pltpu.CompilerParams(vmem_limit_bytes=vmem * 1024 * 1024),
        cost_estimate=pl.CostEstimate(flops=flops, bytes_accessed=moved, transcendentals=0),
    )(*args)


def swap(value, axis, partner):
    return lax.ppermute(value, axis, [(i, partner(i)) for i in range(lax.axis_size(axis))])


def swap_rows(value):
    return swap(value, "x", lambda i: i ^ 1)


def swap_weights(value):
    return swap(value, "x", lambda i: 3 - i)


def swap_core(value):
    return swap(value, "core", lambda i: 1 - i)


def local(patches, upstream, gates, ids, slots, in_weights, out_weights):
    everywhere = ("zlo", "y", "zhi")
    gates, ids, slots = gates.T, ids.T, slots.T
    both = shape((2 * HS, D))
    wi00, wo00 = in_weights[0], out_weights[0]
    wi01, wo01 = swap_weights(wi00), swap_weights(wo00)
    wi10, wo10 = swap_core(wi00), swap_core(wo00)
    sent = call(
        pack_rows_kernel,
        shape((SEND, HALF_W)),
        (gates, ids, slots, patches, upstream),
        500_000_000,
        5_000_000,
        60,
        in_specs=[HBM] * 5,
        out_specs=HBM,
        scratch=[
            pltpu.VMEM((2, T), BF16),
            pltpu.VMEM((2, T), I32),
            pltpu.VMEM((2, T), I32),
            pltpu.VMEM((T, D), BF16),
            pltpu.VMEM((T, D), BF16),
            pltpu.VMEM((SEND, HALF_W), BF16),
            pltpu.SemaphoreType.DMA((5,)),
            pltpu.SemaphoreType.DMA,
        ],
    )
    got = lax.all_to_all(sent, everywhere, split_axis=0, concat_axis=0, tiled=True)
    own = call(
        unpack_rows_kernel,
        shape((2 * ROWS, D)),
        (got,),
        300_000_000,
        2_000_000,
        16,
        in_specs=[HBM],
        scratch=[pltpu.VMEM((SEND, HALF_W), BF16), pltpu.SemaphoreType.DMA((2,))],
    )
    other = swap_rows(own)
    wi11, wo11 = swap_core(wi01), swap_core(wo01)
    hidden = shape((4, ROWS, HS))
    turned = shape((D, 2 * PAD))

    def turn_call(*args):
        return call(turn_kernel, [turned, turned], args, 1_000_000, 5_000_000, 16)

    t_in0, t_out0 = turn_call(wi00, wi10, wo00, wo10)
    t_in1, t_out1 = turn_call(wi01, wi11, wo01, wo11)

    def expert_call(rows):
        return call(
            expert_kernel,
            [shape((ROWS, GW)), hidden, hidden],
            (rows, t_in0, t_in1, t_out0, t_out1, wi00, wi10, wi01, wi11),
            1_100_000_000,
            8_000_000,
            16,
        )

    part_own, pg_own, hid_own = expert_call(own)
    part_other, pg_other, hid_other = expert_call(other)
    part_back = swap_rows(part_other)
    saved = (own, other, pg_own, pg_other, hid_own, hid_other)

    def weight_call(c, *add):
        return call(
            functools.partial(weight_kernel, c, len(add)), both, (*saved, *add), 700_000_000, 4_000_000, 16
        )

    far = swap_core(weight_call(3))
    near = swap_core(weight_call(1))
    far = swap_weights(weight_call(2, far))
    back = call(pack_back_kernel, shape((SEND, QW)), (part_own, part_back), 300_000_000, 2_500_000, 16)
    back = lax.all_to_all(back, everywhere, split_axis=0, concat_axis=0, tiled=True)
    grad_in, grad_out = call(
        last_weight_kernel,
        [shape((HS, D)), shape((HS, D))],
        (*saved, near, far),
        700_000_000,
        6_000_000,
        16,
    )
    patch_grad, gate_grad = call(
        unpack_back_kernel,
        [shape((T, D)), shape((2, T), F32)],
        (back, gates, ids, slots),
        300_000_000,
        1_000_000,
        16,
    )
    return patch_grad, gate_grad.T, grad_in[None], grad_out[None]


def solution(mesh):
    names = ("zlo", "y", "x", "core", "zhi")
    split = Mesh(mesh.devices.reshape(4, 8, 4, 2, 2), names)
    tokens = P(names, None)
    weights = P(("zlo", "y"), ("x", "core", "zhi"), None)
    return jax.shard_map(
        local,
        mesh=split,
        in_specs=(tokens,) * 5 + (weights,) * 2,
        out_specs=(tokens, tokens, weights, weights),
        check_vma=False,
    )
```

```python
import functools

import jax
import jax.numpy as jnp
from jax import lax
from jax.experimental import pallas as pl
from jax.experimental.pallas import tpu as pltpu
from jax.sharding import Mesh, PartitionSpec as P

F32 = jnp.float32
BF16 = jnp.bfloat16
I32 = jnp.int32

CAP = 2
ROOT_TERM = 0.7978845608028654
CUBIC_TERM = 0.044715

T = 128
D = 1664
HS = 208
SRC = 64
ROWS = SRC * CAP
SEND = SRC * 8
PAD = 256
HALF_W = 896
QW = 512
GW = D + 128


def dot(left, right):
    return jnp.dot(left, right, preferred_element_type=F32)


def dot_rows(left, right):
    return lax.dot_general(left, right, (((0,), (0,)), ((), ())), preferred_element_type=F32)


def dot_width(left, right):
    return lax.dot_general(left, right, (((1,), (1,)), ((), ())), preferred_element_type=F32)


def slot_match(ids, slots):
    target = jnp.where(slots >= 0, ids * CAP + slots, -1)
    row = lax.broadcasted_iota(I32, (SEND, T), 0)
    slot = (row >> 4) * CAP + (row & 1)
    return target[0:1, :] == slot, target[1:2, :] == slot, row


def start_copies(pairs, sems):
    copies = [pltpu.make_async_copy(source, place, sems.at[k]) for k, (source, place) in enumerate(pairs)]
    for copy in copies:
        copy.start()
    return copies


def pack_rows_kernel(
    gates_in, ids_in, slots_in, patches_in, upstream_in, out,
    gates, ids, slots, patches, upstream, packed, sems, out_sems,
):
    copies = start_copies(
        [
            (ids_in, ids),
            (slots_in, slots),
            (gates_in, gates),
            (patches_in, patches),
            (upstream_in, upstream),
        ],
        sems,
    )
    for copy in copies[:3]:
        copy.wait()
    m0, m1, row = slot_match(ids[...], slots[...])
    g = gates[...].astype(F32)
    hit = jnp.where(m0 | m1, 1.0, 0.0)
    gate = jnp.where(m0, g[0:1, :], 0.0) + jnp.where(m1, g[1:2, :], 0.0)
    is_up = (row & 2) != 0
    right = (row & 4) != 0
    p_sel = jnp.where(is_up, 0.0, hit)
    u_sel = jnp.where(is_up, gate, 0.0)
    p_l = jnp.where(right, 0.0, p_sel).astype(BF16)
    p_r = jnp.where(right, p_sel, 0.0).astype(BF16)
    u_l = jnp.where(right, 0.0, u_sel).astype(BF16)
    u_r = jnp.where(right, u_sel, 0.0).astype(BF16)
    for copy in copies[3:]:
        copy.wait()
    rest = D - HALF_W
    sent = []
    for half in range(2):
        rows = slice(half * SEND // 2, (half + 1) * SEND // 2)
        place = pl.ds(half * SEND // 2, SEND // 2)
        packed[place, :rest] = (
            dot(p_l[rows], patches[:, :rest])
            + dot(u_l[rows], upstream[:, :rest])
            + dot(p_r[rows], patches[:, HALF_W:])
            + dot(u_r[rows], upstream[:, HALF_W:])
        ).astype(BF16)
        packed[place, rest:] = (
            dot(p_l[rows], patches[:, rest:HALF_W]) + dot(u_l[rows], upstream[:, rest:HALF_W])
        ).astype(BF16)
        sent.append(pltpu.make_async_copy(packed.at[place, :], out.at[place, :], out_sems.at[half]))
        sent[-1].start()
    for copy in sent:
        copy.wait()


def unpack_rows_kernel(got_in, out, got, sems):
    part = 256
    copies = start_copies(
        [(got_in.at[pl.ds(g * part, part), :], got.at[pl.ds(g * part, part), :]) for g in range(SEND // part)], sems
    )
    o = lax.broadcasted_iota(I32, (128, part), 0)
    c = lax.broadcasted_iota(I32, (128, part), 1)
    want = ((o & 63) >> 1) * 8 + (o >> 6) * 2 + (o & 1)
    for g in range(SEND // part):
        copies[g].wait()
        block = got[pl.ds(g * part, part), :]
        for h in range(2):
            sel = jnp.where(c == want + 4 * h, 1.0, 0.0).astype(BF16)
            wide = HALF_W if h == 0 else D - HALF_W
            rows = dot(sel, block[:, :wide]).astype(BF16)
            out[pl.ds(g * 64, 64), pl.ds(h * HALF_W, wide)] = rows[:64]
            out[pl.ds(ROWS + g * 64, 64), pl.ds(h * HALF_W, wide)] = rows[64:]


def gelu_and_slope(value):
    square = value * value
    tangent = jnp.tanh(ROOT_TERM * value * (1.0 + CUBIC_TERM * square))
    up = 0.5 * (1.0 + tangent)
    slope = up + 0.5 * value * (1.0 - tangent * tangent) * ROOT_TERM * (1.0 + 3.0 * CUBIC_TERM * square)
    return value * up, slope


def turn_kernel(in0, in1, out0, out1, in_turned, out_turned):
    for turned, parts in ((in_turned, (in0, in1)), (out_turned, (out0, out1))):
        for k, part in enumerate(parts):
            turned[:, pl.ds(k * PAD, HS)] = part[...].T
            turned[:, pl.ds(k * PAD + HS, PAD - HS)] = jnp.zeros((D, PAD - HS), BF16)


def expert_kernel(rows, t_in0, t_in1, t_out0, t_out1, w0, w1, w2, w3, part, pg_out, hid_out):
    p, u = rows[pl.ds(0, ROWS), :], rows[pl.ds(ROWS, ROWS), :]
    gate = jnp.zeros((ROWS, 1), F32)
    grads = []
    for c, (t_in, t_out) in enumerate(((t_in0, t_out0), (t_in1, t_out1))):
        pre = dot(p, t_in[...])
        back = dot(u, t_out[...])
        hid, slope = gelu_and_slope(pre)
        gate += jnp.sum(hid * back, axis=1, keepdims=True)
        pg = (back * slope).astype(BF16)
        hid = hid.astype(BF16)
        for k in range(2):
            own = slice(k * PAD, k * PAD + HS)
            pg_out[2 * c + k] = pg[:, own]
            hid_out[2 * c + k] = hid[:, own]
            grads.append(pg[:, own])
    total = sum(dot(grad, w[...]) for grad, w in zip(grads, (w0, w1, w2, w3)))
    part[:, :D] = total.astype(BF16)
    lane = lax.broadcasted_iota(I32, (ROWS, 128), 1)
    part[:, D:] = jnp.where(lane == 0, gate, 0.0).astype(BF16)


def weight_grads(c, rows0, rows1, pg0, pg1, hid0, hid1):
    p0, u0 = rows0[pl.ds(0, ROWS), :], rows0[pl.ds(ROWS, ROWS), :]
    p1, u1 = rows1[pl.ds(0, ROWS), :], rows1[pl.ds(ROWS, ROWS), :]
    return (
        dot_rows(pg0[c], p0) + dot_rows(pg1[c], p1),
        dot_rows(hid0[c], u0) + dot_rows(hid1[c], u1),
    )


def weight_kernel(c, add, *refs):
    out = refs[-1]
    grad_in, grad_out = weight_grads(c, *refs[:6])
    if add:
        got = refs[6]
        grad_in += got[pl.ds(0, HS), :].astype(F32)
        grad_out += got[pl.ds(HS, HS), :].astype(F32)
    out[pl.ds(0, HS), :] = grad_in.astype(BF16)
    out[pl.ds(HS, HS), :] = grad_out.astype(BF16)


def weight_sum_kernel(near, far, out_in, out_out):
    out_in[...] = (near[pl.ds(0, HS), :].astype(F32) + far[pl.ds(0, HS), :].astype(F32)).astype(BF16)
    out_out[...] = (near[pl.ds(HS, HS), :].astype(F32) + far[pl.ds(HS, HS), :].astype(F32)).astype(BF16)


def pack_back_kernel(i0, i1, out):
    total = (i0[...].astype(F32) + i1[...].astype(F32)).astype(BF16)
    row = lax.broadcasted_iota(I32, (SEND, ROWS), 0)
    col = lax.broadcasted_iota(I32, (SEND, ROWS), 1)
    want = (row >> 3) * 2 + (row & 1)
    quarter = (row >> 1) & 3
    sels = [jnp.where((col == want) & (quarter == q), 1.0, 0.0).astype(BF16) for q in range(4)]
    last = GW - 3 * QW
    narrow = sum(dot(sels[q], total[:, q * QW : q * QW + last]) for q in range(4))
    wide = sum(dot(sels[q], total[:, q * QW + last : (q + 1) * QW]) for q in range(3))
    out[:, :last] = narrow.astype(BF16)
    out[:, last:] = wide.astype(BF16)


def unpack_back_kernel(got, gates, ids, slots, patch_grad, gate_grad, token):
    token[...] = jnp.zeros_like(token)
    m0, m1, row = slot_match(ids[...], slots[...])
    quarter = (row >> 1) & 3
    hit = jnp.where(m0 | m1, 1.0, 0.0)
    for q in range(4):
        wide = QW if q < 3 else D - 3 * QW
        sel = jnp.where(quarter == q, hit, 0.0).astype(BF16)
        patch_grad[:, pl.ds(q * QW, wide)] = dot_rows(sel, got[:, :wide]).astype(BF16)
    gate_block = got[:, D - 3 * QW : GW - 3 * QW]
    g = gates[...].astype(F32)
    for k, m in enumerate((m0, m1)):
        sel = jnp.where((quarter == 3) & m, 1.0, 0.0).astype(BF16)
        gate_grad[k : k + 1, :] = dot_rows(gate_block, sel)[0:1, :] / g[k : k + 1, :]


def shape(dims, kind=BF16):
    return jax.ShapeDtypeStruct(dims, kind)


ANY = pl.BlockSpec(memory_space=pl.ANY)
HBM = pl.BlockSpec(memory_space=pltpu.HBM)
VM = pl.BlockSpec(memory_space=pltpu.VMEM)


def call(kernel, out_shape, args, flops, moved, vmem, in_specs=None, out_specs=None, scratch=(), after=()):
    used = len(args)

    def body(*refs):
        kernel(*refs[:used], *refs[used + len(after) :])

    return pl.pallas_call(
        body,
        out_shape=out_shape,
        in_specs=(in_specs or [VM] * used) + [ANY] * len(after),
        out_specs=out_specs or jax.tree.map(lambda _: VM, out_shape),
        scratch_shapes=scratch,
        compiler_params=pltpu.CompilerParams(vmem_limit_bytes=vmem * 1024 * 1024),
        cost_estimate=pl.CostEstimate(flops=flops, bytes_accessed=moved, transcendentals=0),
    )(*args, *after)


def swap(value, axis, partner):
    return lax.ppermute(value, axis, [(i, partner(i)) for i in range(lax.axis_size(axis))])


def swap_rows(value):
    return swap(value, "x", lambda i: i ^ 1)


def swap_weights(value):
    return swap(value, "x", lambda i: 3 - i)


def swap_core(value):
    return swap(value, "core", lambda i: 1 - i)


def local(patches, upstream, gates, ids, slots, in_weights, out_weights):
    everywhere = ("zlo", "y", "zhi")
    gates, ids, slots = gates.T, ids.T, slots.T
    both = shape((2 * HS, D))
    wi00, wo00 = in_weights[0], out_weights[0]
    wi01, wo01 = swap_weights(wi00), swap_weights(wo00)
    wi10, wo10 = swap_core(wi00), swap_core(wo00)
    sent = call(
        pack_rows_kernel,
        shape((SEND, HALF_W)),
        (gates, ids, slots, patches, upstream),
        500_000_000,
        5_000_000,
        60,
        in_specs=[HBM] * 5,
        out_specs=HBM,
        scratch=[
            pltpu.VMEM((2, T), BF16),
            pltpu.VMEM((2, T), I32),
            pltpu.VMEM((2, T), I32),
            pltpu.VMEM((T, D), BF16),
            pltpu.VMEM((T, D), BF16),
            pltpu.VMEM((SEND, HALF_W), BF16),
            pltpu.SemaphoreType.DMA((5,)),
            pltpu.SemaphoreType.DMA((2,)),
        ],
    )
    got = lax.all_to_all(sent, everywhere, split_axis=0, concat_axis=0, tiled=True)
    own = call(
        unpack_rows_kernel,
        shape((2 * ROWS, D)),
        (got,),
        300_000_000,
        2_000_000,
        16,
        in_specs=[HBM],
        scratch=[pltpu.VMEM((SEND, HALF_W), BF16), pltpu.SemaphoreType.DMA((2,))],
        after=(wo10,),
    )
    other = swap_rows(own)
    wi11, wo11 = swap_core(wi01), swap_core(wo01)
    hidden = shape((4, ROWS, HS))
    turned = shape((D, 2 * PAD))

    def turn_call(*args):
        return call(turn_kernel, [turned, turned], args, 1_000_000, 5_000_000, 16)

    t_in0, t_out0 = turn_call(wi00, wi10, wo00, wo10)
    t_in1, t_out1 = turn_call(wi01, wi11, wo01, wo11)

    def expert_call(rows):
        return call(
            expert_kernel,
            [shape((ROWS, GW)), hidden, hidden],
            (rows, t_in0, t_in1, t_out0, t_out1, wi00, wi10, wi01, wi11),
            1_100_000_000,
            8_000_000,
            16,
        )

    part_own, pg_own, hid_own = expert_call(own)
    part_other, pg_other, hid_other = expert_call(other)
    part_back = swap_rows(part_other)
    saved = (own, other, pg_own, pg_other, hid_own, hid_other)

    def weight_call(c, add=(), after=()):
        return call(
            functools.partial(weight_kernel, c, len(add)),
            both,
            (*saved, *add),
            700_000_000,
            4_000_000,
            16,
            after=after,
        )

    far = weight_call(2, (swap_core(weight_call(3)),))
    near = swap_core(weight_call(1))
    far = swap_weights(far)
    back = call(pack_back_kernel, shape((SEND, QW)), (part_own, part_back), 300_000_000, 2_500_000, 16)
    back = lax.all_to_all(back, everywhere, split_axis=0, concat_axis=0, tiled=True)
    patch_grad, gate_grad, token = call(
        unpack_back_kernel,
        [shape((T, D)), shape((2, T), F32), shape((8, 128), F32)],
        (back, gates, ids, slots),
        300_000_000,
        1_000_000,
        16,
    )
    near = weight_call(0, (near,), (token,))
    grad_in, grad_out = call(
        weight_sum_kernel, [shape((HS, D))] * 2, (near, far), 1_000_000, 4_000_000, 16
    )
    return patch_grad, gate_grad.T, grad_in[None], grad_out[None]


def solution(mesh):
    names = ("zlo", "y", "x", "core", "zhi")
    split = Mesh(mesh.devices.reshape(4, 8, 4, 2, 2), names)
    tokens = P(names, None)
    weights = P(("zlo", "y"), ("x", "core", "zhi"), None)
    return jax.shard_map(
        local,
        mesh=split,
        in_specs=(tokens,) * 5 + (weights,) * 2,
        out_specs=(tokens, tokens, weights, weights),
        check_vma=False,
    )
```

```python
import functools

import jax
import jax.numpy as jnp
from jax import lax
from jax.experimental import pallas as pl
from jax.experimental.pallas import tpu as pltpu
from jax.sharding import Mesh, PartitionSpec as P

F32 = jnp.float32
BF16 = jnp.bfloat16
I32 = jnp.int32

CAP = 2
ROOT_TERM = 0.7978845608028654
CUBIC_TERM = 0.044715

T = 128
D = 1664
HS = 208
SRC = 64
ROWS = SRC * CAP
PAD = 256
GW = D + 128
SEND_BLOCKS = D // 128
BACK_BLOCKS = GW // 128


def dot(left, right):
    return jnp.dot(left, right, preferred_element_type=F32)


def dot_rows(left, right):
    return lax.dot_general(left, right, (((0,), (0,)), ((), ())), preferred_element_type=F32)


def dot_width(left, right):
    return lax.dot_general(left, right, (((1,), (1,)), ((), ())), preferred_element_type=F32)


def slot_match(ids, slots, per):
    target = jnp.where(slots >= 0, ids * CAP + slots, -1)
    row = lax.broadcasted_iota(I32, (SRC * per, T), 0)
    slot = row // (2 * per) * CAP + (row & 1)
    return target[0:1, :] == slot, target[1:2, :] == slot, row


def start_copies(pairs, sems):
    copies = [pltpu.make_async_copy(source, place, sems.at[k]) for k, (source, place) in enumerate(pairs)]
    for copy in copies:
        copy.start()
    return copies


def pack_rows_kernel(
    gates_in, ids_in, slots_in, patches_in, upstream_in, out,
    gates, ids, slots, patches, upstream, packed, sems, out_sems,
):
    copies = start_copies(
        [
            (ids_in, ids),
            (slots_in, slots),
            (gates_in, gates),
            (patches_in, patches),
            (upstream_in, upstream),
        ],
        sems,
    )
    for copy in copies[:3]:
        copy.wait()
    m0, m1, row = slot_match(ids[...], slots[...], 4)
    g = gates[...].astype(F32)
    gate = jnp.where(m0, g[0:1, :], 0.0) + jnp.where(m1, g[1:2, :], 0.0)
    is_up = (row & 2) != 0
    p_sel = jnp.where(is_up, 0.0, jnp.where(m0 | m1, 1.0, 0.0)).astype(BF16)
    u_sel = jnp.where(is_up, gate, 0.0).astype(BF16)
    for copy in copies[3:]:
        copy.wait()
    sent = []
    for half in range(2):
        part = SRC // 2
        rows = slice(half * part * 4, (half + 1) * part * 4)
        filled = (dot(p_sel[rows], patches[...]) + dot(u_sel[rows], upstream[...])).astype(BF16)
        place = pl.ds(half * part, part)
        for j in range(SEND_BLOCKS):
            packed[place, j] = filled[:, j * 128 : (j + 1) * 128].reshape(part, 4, 128)
        sent.append(pltpu.make_async_copy(packed.at[place], out.at[place], out_sems.at[half]))
        sent[-1].start()
    for copy in sent:
        copy.wait()


def unpack_rows_kernel(got_in, out, got, rows, sems):
    part = SRC // 2
    copies = start_copies([(got_in.at[pl.ds(g * part, part)], got.at[pl.ds(g * part, part)]) for g in range(2)], sems)
    o = lax.broadcasted_iota(I32, (2 * ROWS, 4 * SRC), 0)
    c = lax.broadcasted_iota(I32, (2 * ROWS, 4 * SRC), 1)
    want = ((o & (ROWS - 1)) >> 1) * 4 + o // ROWS * 2 + (o & 1)
    sel = jnp.where(c == want, 1.0, 0.0).astype(BF16)
    for g in range(2):
        copies[g].wait()
        for j in range(SEND_BLOCKS):
            block = got[pl.ds(g * part, part), j].reshape(part * 4, 128)
            rows[pl.ds(g * part * 4, part * 4), pl.ds(j * 128, 128)] = block
    out[...] = dot(sel, rows[...]).astype(BF16)


def gelu_and_slope(value):
    square = value * value
    tangent = jnp.tanh(ROOT_TERM * value * (1.0 + CUBIC_TERM * square))
    up = 0.5 * (1.0 + tangent)
    slope = up + 0.5 * value * (1.0 - tangent * tangent) * ROOT_TERM * (1.0 + 3.0 * CUBIC_TERM * square)
    return value * up, slope


def turn_kernel(in0, in1, out0, out1, in_turned, out_turned):
    for turned, parts in ((in_turned, (in0, in1)), (out_turned, (out0, out1))):
        for k, part in enumerate(parts):
            turned[:, pl.ds(k * PAD, HS)] = part[...].T
            turned[:, pl.ds(k * PAD + HS, PAD - HS)] = jnp.zeros((D, PAD - HS), BF16)


def expert_kernel(rows, t_in0, t_in1, t_out0, t_out1, w0, w1, w2, w3, part, pg_out, hid_out):
    p, u = rows[pl.ds(0, ROWS), :], rows[pl.ds(ROWS, ROWS), :]
    gate = jnp.zeros((ROWS, 1), F32)
    grads = []
    for c, (t_in, t_out) in enumerate(((t_in0, t_out0), (t_in1, t_out1))):
        pre = dot(p, t_in[...])
        back = dot(u, t_out[...])
        hid, slope = gelu_and_slope(pre)
        gate += jnp.sum(hid * back, axis=1, keepdims=True)
        pg = (back * slope).astype(BF16)
        hid = hid.astype(BF16)
        for k in range(2):
            own = slice(k * PAD, k * PAD + HS)
            pg_out[2 * c + k] = pg[:, own]
            hid_out[2 * c + k] = hid[:, own]
            grads.append(pg[:, own])
    total = sum(dot(grad, w[...]) for grad, w in zip(grads, (w0, w1, w2, w3)))
    part[:, :D] = total.astype(BF16)
    lane = lax.broadcasted_iota(I32, (ROWS, 128), 1)
    part[:, D:] = jnp.where(lane == 0, gate, 0.0).astype(BF16)


def weight_grads(c, rows0, rows1, pg0, pg1, hid0, hid1):
    p0, u0 = rows0[pl.ds(0, ROWS), :], rows0[pl.ds(ROWS, ROWS), :]
    p1, u1 = rows1[pl.ds(0, ROWS), :], rows1[pl.ds(ROWS, ROWS), :]
    return (
        dot_rows(pg0[c], p0) + dot_rows(pg1[c], p1),
        dot_rows(hid0[c], u0) + dot_rows(hid1[c], u1),
    )


def weight_kernel(c, add, *refs):
    out = refs[-1]
    grad_in, grad_out = weight_grads(c, *refs[:6])
    if add:
        got = refs[6]
        grad_in += got[pl.ds(0, HS), :].astype(F32)
        grad_out += got[pl.ds(HS, HS), :].astype(F32)
    out[pl.ds(0, HS), :] = grad_in.astype(BF16)
    out[pl.ds(HS, HS), :] = grad_out.astype(BF16)


def weight_sum_kernel(near, far, out_in, out_out):
    out_in[...] = (near[pl.ds(0, HS), :].astype(F32) + far[pl.ds(0, HS), :].astype(F32)).astype(BF16)
    out_out[...] = (near[pl.ds(HS, HS), :].astype(F32) + far[pl.ds(HS, HS), :].astype(F32)).astype(BF16)


def pack_back_kernel(i0, i1, out):
    total = (i0[...].astype(F32) + i1[...].astype(F32)).astype(BF16)
    for j in range(BACK_BLOCKS):
        out[:, j] = total[:, j * 128 : (j + 1) * 128].reshape(SRC, CAP, 128)


def unpack_back_kernel(got, gates, ids, slots, patch_grad, gate_grad, token):
    token[...] = jnp.zeros_like(token)
    m0, m1, _ = slot_match(ids[...], slots[...], CAP)
    sel = jnp.where(m0 | m1, 1.0, 0.0).astype(BF16)
    for j in range(SEND_BLOCKS):
        rows = got[:, j].reshape(ROWS, 128)
        patch_grad[:, pl.ds(j * 128, 128)] = dot_rows(sel, rows).astype(BF16)
    gate_block = got[:, SEND_BLOCKS].reshape(ROWS, 128)
    g = gates[...].astype(F32)
    for k, m in enumerate((m0, m1)):
        sel = jnp.where(m, 1.0, 0.0).astype(BF16)
        gate_grad[k : k + 1, :] = dot_rows(gate_block, sel)[0:1, :] / g[k : k + 1, :]


def shape(dims, kind=BF16):
    return jax.ShapeDtypeStruct(dims, kind)


ANY = pl.BlockSpec(memory_space=pl.ANY)
HBM = pl.BlockSpec(memory_space=pltpu.HBM)
VM = pl.BlockSpec(memory_space=pltpu.VMEM)


def call(kernel, out_shape, args, flops, moved, vmem, in_specs=None, out_specs=None, scratch=(), after=()):
    used = len(args)

    def body(*refs):
        kernel(*refs[:used], *refs[used + len(after) :])

    return pl.pallas_call(
        body,
        out_shape=out_shape,
        in_specs=(in_specs or [VM] * used) + [ANY] * len(after),
        out_specs=out_specs or jax.tree.map(lambda _: VM, out_shape),
        scratch_shapes=scratch,
        compiler_params=pltpu.CompilerParams(vmem_limit_bytes=vmem * 1024 * 1024),
        cost_estimate=pl.CostEstimate(flops=flops, bytes_accessed=moved, transcendentals=0),
    )(*args, *after)


def swap(value, axis, partner):
    return lax.ppermute(value, axis, [(i, partner(i)) for i in range(lax.axis_size(axis))])


def swap_rows(value):
    return swap(value, "x", lambda i: i ^ 1)


def swap_weights(value):
    return swap(value, "x", lambda i: 3 - i)


def swap_core(value):
    return swap(value, "core", lambda i: 1 - i)


def local(patches, upstream, gates, ids, slots, in_weights, out_weights):
    everywhere = ("zlo", "y", "zhi")
    gates, ids, slots = gates.T, ids.T, slots.T
    both = shape((2 * HS, D))
    wi00, wo00 = in_weights[0], out_weights[0]
    wi01, wo01 = swap_weights(wi00), swap_weights(wo00)
    wi10, wo10 = swap_core(wi00), swap_core(wo00)
    sent = call(
        pack_rows_kernel,
        shape((SRC, SEND_BLOCKS, 4, 128)),
        (gates, ids, slots, patches, upstream),
        500_000_000,
        5_000_000,
        60,
        in_specs=[HBM] * 5,
        out_specs=HBM,
        scratch=[
            pltpu.VMEM((2, T), BF16),
            pltpu.VMEM((2, T), I32),
            pltpu.VMEM((2, T), I32),
            pltpu.VMEM((T, D), BF16),
            pltpu.VMEM((T, D), BF16),
            pltpu.VMEM((SRC, SEND_BLOCKS, 4, 128), BF16),
            pltpu.SemaphoreType.DMA((5,)),
            pltpu.SemaphoreType.DMA((2,)),
        ],
    )
    got = lax.all_to_all(sent, everywhere, split_axis=0, concat_axis=0, tiled=True)
    own = call(
        unpack_rows_kernel,
        shape((2 * ROWS, D)),
        (got,),
        300_000_000,
        2_000_000,
        16,
        in_specs=[HBM],
        scratch=[
            pltpu.VMEM((SRC, SEND_BLOCKS, 4, 128), BF16),
            pltpu.VMEM((4 * SRC, D), BF16),
            pltpu.SemaphoreType.DMA((2,)),
        ],
    )
    other = swap_rows(own)
    wi11, wo11 = swap_core(wi01), swap_core(wo01)
    hidden = shape((4, ROWS, HS))
    turned = shape((D, 2 * PAD))

    def turn_call(*args):
        return call(turn_kernel, [turned, turned], args, 1_000_000, 5_000_000, 16)

    t_in0, t_out0 = turn_call(wi00, wi10, wo00, wo10)
    t_in1, t_out1 = turn_call(wi01, wi11, wo01, wo11)

    def expert_call(rows):
        return call(
            expert_kernel,
            [shape((ROWS, GW)), hidden, hidden],
            (rows, t_in0, t_in1, t_out0, t_out1, wi00, wi10, wi01, wi11),
            1_100_000_000,
            8_000_000,
            16,
        )

    part_own, pg_own, hid_own = expert_call(own)
    part_other, pg_other, hid_other = expert_call(other)
    part_back = swap_rows(part_other)
    saved = (own, other, pg_own, pg_other, hid_own, hid_other)

    def weight_call(c, add=(), after=()):
        return call(
            functools.partial(weight_kernel, c, len(add)),
            both,
            (*saved, *add),
            700_000_000,
            4_000_000,
            16,
            after=after,
        )

    far = weight_call(2, (swap_core(weight_call(3)),))
    near = swap_core(weight_call(1))
    far = swap_weights(far)
    back = call(pack_back_kernel, shape((SRC, BACK_BLOCKS, CAP, 128)), (part_own, part_back), 300_000_000, 2_500_000, 16)
    back = lax.all_to_all(back, everywhere, split_axis=0, concat_axis=0, tiled=True)
    patch_grad, gate_grad, token = call(
        unpack_back_kernel,
        [shape((T, D)), shape((2, T), F32), shape((8, 128), F32)],
        (back, gates, ids, slots),
        300_000_000,
        1_000_000,
        16,
    )
    near = weight_call(0, (near,), (token,))
    grad_in, grad_out = call(
        weight_sum_kernel, [shape((HS, D))] * 2, (near, far), 1_000_000, 4_000_000, 16
    )
    return patch_grad, gate_grad.T, grad_in[None], grad_out[None]


def solution(mesh):
    names = ("zlo", "y", "x", "core", "zhi")
    split = Mesh(mesh.devices.reshape(4, 8, 4, 2, 2), names)
    tokens = P(names, None)
    weights = P(("zlo", "y"), ("x", "core", "zhi"), None)
    return jax.shard_map(
        local,
        mesh=split,
        in_specs=(tokens,) * 5 + (weights,) * 2,
        out_specs=(tokens, tokens, weights, weights),
        check_vma=False,
    )
```

```python
import functools

import jax
import jax.numpy as jnp
from jax import lax
from jax.experimental import pallas as pl
from jax.experimental.pallas import tpu as pltpu
from jax.sharding import Mesh, PartitionSpec as P

F32 = jnp.float32
BF16 = jnp.bfloat16
I32 = jnp.int32

CAP = 2
ROOT_TERM = 0.7978845608028654
CUBIC_TERM = 0.044715

T = 128
D = 1664
HS = 208
SRC = 64
ROWS = SRC * CAP
PAD = 256
GW = D + 128
SEND_BLOCKS = D // 128
BACK_BLOCKS = GW // 128


def dot(left, right):
    return jnp.dot(left, right, preferred_element_type=F32)


def dot_rows(left, right):
    return lax.dot_general(left, right, (((0,), (0,)), ((), ())), preferred_element_type=F32)


def dot_width(left, right):
    return lax.dot_general(left, right, (((1,), (1,)), ((), ())), preferred_element_type=F32)


def slot_match(ids, slots, per):
    target = jnp.where(slots >= 0, ids * CAP + slots, -1)
    row = lax.broadcasted_iota(I32, (SRC * per, T), 0)
    slot = row // (2 * per) * CAP + (row & 1)
    return target[0:1, :] == slot, target[1:2, :] == slot, row


def start_copies(pairs, sems):
    copies = [pltpu.make_async_copy(source, place, sems.at[k]) for k, (source, place) in enumerate(pairs)]
    for copy in copies:
        copy.start()
    return copies


def pack_rows_kernel(
    gates_in, ids_in, slots_in, patches_in, upstream_in, out,
    gates, ids, slots, patches, upstream, packed, sems, out_sems,
):
    copies = start_copies(
        [
            (ids_in, ids),
            (slots_in, slots),
            (gates_in, gates),
            (patches_in, patches),
            (upstream_in, upstream),
        ],
        sems,
    )
    for copy in copies[:3]:
        copy.wait()
    m0, m1, row = slot_match(ids[...], slots[...], 4)
    g = gates[...].astype(F32)
    gate = jnp.where(m0, g[0:1, :], 0.0) + jnp.where(m1, g[1:2, :], 0.0)
    is_up = (row & 2) != 0
    p_sel = jnp.where(is_up, 0.0, jnp.where(m0 | m1, 1.0, 0.0)).astype(BF16)
    u_sel = jnp.where(is_up, gate, 0.0).astype(BF16)
    for copy in copies[3:]:
        copy.wait()
    sent = []
    for half in range(2):
        part = SRC // 2
        rows = slice(half * part * 4, (half + 1) * part * 4)
        filled = (dot(p_sel[rows], patches[...]) + dot(u_sel[rows], upstream[...])).astype(BF16)
        place = pl.ds(half * part, part)
        for j in range(SEND_BLOCKS):
            packed[place, j] = filled[:, j * 128 : (j + 1) * 128].reshape(part, 4, 128)
        sent.append(pltpu.make_async_copy(packed.at[place], out.at[place], out_sems.at[half]))
        sent[-1].start()
    for copy in sent:
        copy.wait()


def unpack_rows_kernel(got_in, out, got, rows, sems):
    part = SRC // 2
    copies = start_copies([(got_in.at[pl.ds(g * part, part)], got.at[pl.ds(g * part, part)]) for g in range(2)], sems)
    o = lax.broadcasted_iota(I32, (2 * ROWS, 4 * SRC), 0)
    c = lax.broadcasted_iota(I32, (2 * ROWS, 4 * SRC), 1)
    want = ((o & (ROWS - 1)) >> 1) * 4 + o // ROWS * 2 + (o & 1)
    sel = jnp.where(c == want, 1.0, 0.0).astype(BF16)
    for g in range(2):
        copies[g].wait()
        for j in range(SEND_BLOCKS):
            block = got[pl.ds(g * part, part), j].reshape(part * 4, 128)
            rows[pl.ds(g * part * 4, part * 4), pl.ds(j * 128, 128)] = block
    out[...] = dot(sel, rows[...]).astype(BF16)


def gelu_and_slope(value):
    square = value * value
    tangent = jnp.tanh(ROOT_TERM * value * (1.0 + CUBIC_TERM * square))
    up = 0.5 * (1.0 + tangent)
    slope = up + 0.5 * value * (1.0 - tangent * tangent) * ROOT_TERM * (1.0 + 3.0 * CUBIC_TERM * square)
    return value * up, slope


def turn_kernel(in0, in1, out0, out1, in_turned, out_turned):
    for turned, parts in ((in_turned, (in0, in1)), (out_turned, (out0, out1))):
        for k, part in enumerate(parts):
            turned[:, pl.ds(k * PAD, HS)] = part[...].T
            turned[:, pl.ds(k * PAD + HS, PAD - HS)] = jnp.zeros((D, PAD - HS), BF16)


def expert_kernel(rows, t_in0, t_in1, t_out0, t_out1, w0, w1, w2, w3, part, pg_out, hid_out):
    p, u = rows[pl.ds(0, ROWS), :], rows[pl.ds(ROWS, ROWS), :]
    gate = jnp.zeros((ROWS, 1), F32)
    grads = []
    for c, (t_in, t_out) in enumerate(((t_in0, t_out0), (t_in1, t_out1))):
        pre = dot(p, t_in[...])
        back = dot(u, t_out[...])
        hid, slope = gelu_and_slope(pre)
        gate += jnp.sum(hid * back, axis=1, keepdims=True)
        pg = (back * slope).astype(BF16)
        hid = hid.astype(BF16)
        for k in range(2):
            own = slice(k * PAD, k * PAD + HS)
            pg_out[2 * c + k] = pg[:, own]
            hid_out[2 * c + k] = hid[:, own]
            grads.append(pg[:, own])
    total = sum(dot(grad, w[...]) for grad, w in zip(grads, (w0, w1, w2, w3)))
    part[:, :D] = total.astype(BF16)
    lane = lax.broadcasted_iota(I32, (ROWS, 128), 1)
    part[:, D:] = jnp.where(lane == 0, gate, 0.0).astype(BF16)


def weight_grads(c, rows0, rows1, pg0, pg1, hid0, hid1):
    p0, u0 = rows0[pl.ds(0, ROWS), :], rows0[pl.ds(ROWS, ROWS), :]
    p1, u1 = rows1[pl.ds(0, ROWS), :], rows1[pl.ds(ROWS, ROWS), :]
    return (
        dot_rows(pg0[c], p0) + dot_rows(pg1[c], p1),
        dot_rows(hid0[c], u0) + dot_rows(hid1[c], u1),
    )


def weight_kernel(c, add, *refs):
    out = refs[-1]
    grad_in, grad_out = weight_grads(c, *refs[:6])
    if add:
        got = refs[6]
        grad_in += got[pl.ds(0, HS), :].astype(F32)
        grad_out += got[pl.ds(HS, HS), :].astype(F32)
    out[pl.ds(0, HS), :] = grad_in.astype(BF16)
    out[pl.ds(HS, HS), :] = grad_out.astype(BF16)


def partial_sum_kernel(own, far, out):
    out[...] = (own[...].astype(F32) + far[...].astype(F32)).astype(BF16)


def weight_sum_kernel(own, near, out_in, out_out):
    for k, out in enumerate((out_in, out_out)):
        rows = pl.ds(k * HS, HS)
        out[...] = (own[rows, :].astype(F32) + near[rows, :].astype(F32)).astype(BF16)


def pack_back_kernel(i0, i1, out):
    total = (i0[...].astype(F32) + i1[...].astype(F32)).astype(BF16)
    for j in range(BACK_BLOCKS):
        out[:, j] = total[:, j * 128 : (j + 1) * 128].reshape(SRC, CAP, 128)


def unpack_back_kernel(got, gates, ids, slots, patch_grad, gate_grad, token):
    token[...] = jnp.zeros_like(token)
    m0, m1, _ = slot_match(ids[...], slots[...], CAP)
    sel = jnp.where(m0 | m1, 1.0, 0.0).astype(BF16)
    for j in range(SEND_BLOCKS):
        rows = got[:, j].reshape(ROWS, 128)
        patch_grad[:, pl.ds(j * 128, 128)] = dot_rows(sel, rows).astype(BF16)
    gate_block = got[:, SEND_BLOCKS].reshape(ROWS, 128)
    g = gates[...].astype(F32)
    for k, m in enumerate((m0, m1)):
        sel = jnp.where(m, 1.0, 0.0).astype(BF16)
        gate_grad[k : k + 1, :] = dot_rows(gate_block, sel)[0:1, :] / g[k : k + 1, :]


def shape(dims, kind=BF16):
    return jax.ShapeDtypeStruct(dims, kind)


ANY = pl.BlockSpec(memory_space=pl.ANY)
HBM = pl.BlockSpec(memory_space=pltpu.HBM)
VM = pl.BlockSpec(memory_space=pltpu.VMEM)


def call(kernel, out_shape, args, flops, moved, vmem, in_specs=None, out_specs=None, scratch=(), after=()):
    used = len(args)

    def body(*refs):
        kernel(*refs[:used], *refs[used + len(after) :])

    return pl.pallas_call(
        body,
        out_shape=out_shape,
        in_specs=(in_specs or [VM] * used) + [ANY] * len(after),
        out_specs=out_specs or jax.tree.map(lambda _: VM, out_shape),
        scratch_shapes=scratch,
        compiler_params=pltpu.CompilerParams(vmem_limit_bytes=vmem * 1024 * 1024),
        cost_estimate=pl.CostEstimate(flops=flops, bytes_accessed=moved, transcendentals=0),
    )(*args, *after)


def swap(value, axis, partner):
    return lax.ppermute(value, axis, [(i, partner(i)) for i in range(lax.axis_size(axis))])


def swap_rows(value):
    return swap(value, "x", lambda i: i ^ 1)


def swap_weights(value):
    return swap(value, "x", lambda i: 3 - i)


def swap_core(value):
    return swap(value, "core", lambda i: 1 - i)


def local(patches, upstream, gates, ids, slots, in_weights, out_weights):
    everywhere = ("zlo", "y", "zhi")
    gates, ids, slots = gates.T, ids.T, slots.T
    both = shape((2 * HS, D))
    wi00, wo00 = in_weights[0], out_weights[0]
    wi01, wo01 = swap_weights(wi00), swap_weights(wo00)
    wi10, wo10 = swap_core(wi00), swap_core(wo00)
    sent = call(
        pack_rows_kernel,
        shape((SRC, SEND_BLOCKS, 4, 128)),
        (gates, ids, slots, patches, upstream),
        500_000_000,
        5_000_000,
        60,
        in_specs=[HBM] * 5,
        out_specs=HBM,
        scratch=[
            pltpu.VMEM((2, T), BF16),
            pltpu.VMEM((2, T), I32),
            pltpu.VMEM((2, T), I32),
            pltpu.VMEM((T, D), BF16),
            pltpu.VMEM((T, D), BF16),
            pltpu.VMEM((SRC, SEND_BLOCKS, 4, 128), BF16),
            pltpu.SemaphoreType.DMA((5,)),
            pltpu.SemaphoreType.DMA((2,)),
        ],
    )
    got = lax.all_to_all(sent, everywhere, split_axis=0, concat_axis=0, tiled=True)
    own = call(
        unpack_rows_kernel,
        shape((2 * ROWS, D)),
        (got,),
        300_000_000,
        2_000_000,
        16,
        in_specs=[HBM],
        scratch=[
            pltpu.VMEM((SRC, SEND_BLOCKS, 4, 128), BF16),
            pltpu.VMEM((4 * SRC, D), BF16),
            pltpu.SemaphoreType.DMA((2,)),
        ],
    )
    other = swap_rows(own)
    wi11, wo11 = swap_core(wi01), swap_core(wo01)
    hidden = shape((4, ROWS, HS))
    turned = shape((D, 2 * PAD))

    def turn_call(*args):
        return call(turn_kernel, [turned, turned], args, 1_000_000, 5_000_000, 16)

    t_in0, t_out0 = turn_call(wi00, wi10, wo00, wo10)
    t_in1, t_out1 = turn_call(wi01, wi11, wo01, wo11)

    def expert_call(rows):
        return call(
            expert_kernel,
            [shape((ROWS, GW)), hidden, hidden],
            (rows, t_in0, t_in1, t_out0, t_out1, wi00, wi10, wi01, wi11),
            1_100_000_000,
            8_000_000,
            16,
        )

    part_own, pg_own, hid_own = expert_call(own)
    part_other, pg_other, hid_other = expert_call(other)
    part_back = swap_rows(part_other)
    saved = (own, other, pg_own, pg_other, hid_own, hid_other)

    def weight_call(c, add=(), after=()):
        return call(
            functools.partial(weight_kernel, c, len(add)),
            both,
            (*saved, *add),
            700_000_000,
            4_000_000,
            16,
            after=after,
        )

    far = weight_call(2, (swap_core(weight_call(3)),))
    sent = far
    far = swap_weights(far)
    near = swap_core(weight_call(1, after=(sent,)))
    back = call(pack_back_kernel, shape((SRC, BACK_BLOCKS, CAP, 128)), (part_own, part_back), 300_000_000, 2_500_000, 16)
    back = lax.all_to_all(back, everywhere, split_axis=0, concat_axis=0, tiled=True)
    patch_grad, gate_grad, token = call(
        unpack_back_kernel,
        [shape((T, D)), shape((2, T), F32), shape((8, 128), F32)],
        (back, gates, ids, slots),
        300_000_000,
        1_000_000,
        16,
    )
    mine = weight_call(0, after=(token,))
    mine = call(partial_sum_kernel, both, (mine, far), 1_000_000, 4_000_000, 16, after=(token,))
    grad_in, grad_out = call(
        weight_sum_kernel, [shape((HS, D))] * 2, (mine, near), 1_000_000, 4_000_000, 16, after=(token,)
    )
    return patch_grad, gate_grad.T, grad_in[None], grad_out[None]


def solution(mesh):
    names = ("zlo", "y", "x", "core", "zhi")
    split = Mesh(mesh.devices.reshape(4, 8, 4, 2, 2), names)
    tokens = P(names, None)
    weights = P(("zlo", "y"), ("x", "core", "zhi"), None)
    return jax.shard_map(
        local,
        mesh=split,
        in_specs=(tokens,) * 5 + (weights,) * 2,
        out_specs=(tokens, tokens, weights, weights),
        check_vma=False,
    )
```

```python
import functools

import jax
import jax.numpy as jnp
from jax import lax
from jax.experimental import pallas as pl
from jax.experimental.pallas import tpu as pltpu
from jax.sharding import Mesh, PartitionSpec as P

F32 = jnp.float32
BF16 = jnp.bfloat16
I32 = jnp.int32

CAP = 2
ROOT_TERM = 0.7978845608028654
CUBIC_TERM = 0.044715

T = 128
D = 1664
HS = 208
SRC = 64
ROWS = SRC * CAP
PAD = 256
GW = D + 128
SEND_BLOCKS = D // 128
BACK_BLOCKS = GW // 128


def dot(left, right):
    return jnp.dot(left, right, preferred_element_type=F32)


def dot_rows(left, right):
    return lax.dot_general(left, right, (((0,), (0,)), ((), ())), preferred_element_type=F32)


def dot_width(left, right):
    return lax.dot_general(left, right, (((1,), (1,)), ((), ())), preferred_element_type=F32)


def slot_match(ids, slots, per):
    target = jnp.where(slots >= 0, ids * CAP + slots, -1)
    row = lax.broadcasted_iota(I32, (SRC * per, T), 0)
    slot = row // (2 * per) * CAP + (row & 1)
    return target[0:1, :] == slot, target[1:2, :] == slot, row


def start_copies(pairs, sems):
    copies = [pltpu.make_async_copy(source, place, sems.at[k]) for k, (source, place) in enumerate(pairs)]
    for copy in copies:
        copy.start()
    return copies


def pack_rows_kernel(
    gates_in, ids_in, slots_in, patches_in, upstream_in, out,
    gates, ids, slots, patches, upstream, packed, sems, out_sems,
):
    copies = start_copies(
        [
            (ids_in, ids),
            (slots_in, slots),
            (gates_in, gates),
            (patches_in, patches),
            (upstream_in, upstream),
        ],
        sems,
    )
    for copy in copies[:3]:
        copy.wait()
    m0, m1, row = slot_match(ids[...], slots[...], 4)
    g = gates[...].astype(F32)
    gate = jnp.where(m0, g[0:1, :], 0.0) + jnp.where(m1, g[1:2, :], 0.0)
    is_up = (row & 2) != 0
    p_sel = jnp.where(is_up, 0.0, jnp.where(m0 | m1, 1.0, 0.0)).astype(BF16)
    u_sel = jnp.where(is_up, gate, 0.0).astype(BF16)
    for copy in copies[3:]:
        copy.wait()
    sent = []
    for half in range(2):
        part = SRC // 2
        rows = slice(half * part * 4, (half + 1) * part * 4)
        filled = (dot(p_sel[rows], patches[...]) + dot(u_sel[rows], upstream[...])).astype(BF16)
        place = pl.ds(half * part, part)
        for j in range(SEND_BLOCKS):
            packed[place, j] = filled[:, j * 128 : (j + 1) * 128].reshape(part, 4, 128)
        sent.append(pltpu.make_async_copy(packed.at[place], out.at[place], out_sems.at[half]))
        sent[-1].start()
    for copy in sent:
        copy.wait()


def unpack_rows_kernel(got_in, out, got, rows, sems):
    part = SRC // 2
    copies = start_copies([(got_in.at[pl.ds(g * part, part)], got.at[pl.ds(g * part, part)]) for g in range(2)], sems)
    o = lax.broadcasted_iota(I32, (2 * ROWS, 4 * SRC), 0)
    c = lax.broadcasted_iota(I32, (2 * ROWS, 4 * SRC), 1)
    want = ((o & (ROWS - 1)) >> 1) * 4 + o // ROWS * 2 + (o & 1)
    sel = jnp.where(c == want, 1.0, 0.0).astype(BF16)
    for g in range(2):
        copies[g].wait()
        for j in range(SEND_BLOCKS):
            block = got[pl.ds(g * part, part), j].reshape(part * 4, 128)
            rows[pl.ds(g * part * 4, part * 4), pl.ds(j * 128, 128)] = block
    out[...] = dot(sel, rows[...]).astype(BF16)


def gelu_and_slope(value):
    square = value * value
    tangent = jnp.tanh(ROOT_TERM * value * (1.0 + CUBIC_TERM * square))
    up = 0.5 * (1.0 + tangent)
    slope = up + 0.5 * value * (1.0 - tangent * tangent) * ROOT_TERM * (1.0 + 3.0 * CUBIC_TERM * square)
    return value * up, slope


def turn_kernel(in0, in1, out0, out1, in_turned, out_turned):
    for turned, parts in ((in_turned, (in0, in1)), (out_turned, (out0, out1))):
        for k, part in enumerate(parts):
            turned[:, pl.ds(k * PAD, HS)] = part[...].T
            turned[:, pl.ds(k * PAD + HS, PAD - HS)] = jnp.zeros((D, PAD - HS), BF16)


def expert_kernel(rows, t_in0, t_in1, t_out0, t_out1, w0, w1, w2, w3, part, pg_out, hid_out):
    p, u = rows[pl.ds(0, ROWS), :], rows[pl.ds(ROWS, ROWS), :]
    gate = jnp.zeros((ROWS, 1), F32)
    grads = []
    for c, (t_in, t_out) in enumerate(((t_in0, t_out0), (t_in1, t_out1))):
        pre = dot(p, t_in[...])
        back = dot(u, t_out[...])
        hid, slope = gelu_and_slope(pre)
        gate += jnp.sum(hid * back, axis=1, keepdims=True)
        pg = (back * slope).astype(BF16)
        hid = hid.astype(BF16)
        for k in range(2):
            own = slice(k * PAD, k * PAD + HS)
            pg_out[2 * c + k] = pg[:, own]
            hid_out[2 * c + k] = hid[:, own]
            grads.append(pg[:, own])
    total = sum(dot(grad, w[...]) for grad, w in zip(grads, (w0, w1, w2, w3)))
    part[:, :D] = total.astype(BF16)
    lane = lax.broadcasted_iota(I32, (ROWS, 128), 1)
    part[:, D:] = jnp.where(lane == 0, gate, 0.0).astype(BF16)


def weight_grads(c, rows0, rows1, pg0, pg1, hid0, hid1):
    p0, u0 = rows0[pl.ds(0, ROWS), :], rows0[pl.ds(ROWS, ROWS), :]
    p1, u1 = rows1[pl.ds(0, ROWS), :], rows1[pl.ds(ROWS, ROWS), :]
    return (
        dot_rows(pg0[c], p0) + dot_rows(pg1[c], p1),
        dot_rows(hid0[c], u0) + dot_rows(hid1[c], u1),
    )


def weight_kernel(c, add, *refs):
    out = refs[-1]
    grad_in, grad_out = weight_grads(c, *refs[:6])
    if add:
        got = refs[6]
        grad_in += got[pl.ds(0, HS), :].astype(F32)
        grad_out += got[pl.ds(HS, HS), :].astype(F32)
    out[pl.ds(0, HS), :] = grad_in.astype(BF16)
    out[pl.ds(HS, HS), :] = grad_out.astype(BF16)


def partial_sum_kernel(own, far, out):
    out[...] = (own[...].astype(F32) + far[...].astype(F32)).astype(BF16)


def weight_sum_kernel(own, near, out_in, out_out):
    for k, out in enumerate((out_in, out_out)):
        rows = pl.ds(k * HS, HS)
        out[...] = (own[rows, :].astype(F32) + near[rows, :].astype(F32)).astype(BF16)


def pack_back_kernel(i0, i1, out):
    total = (i0[...].astype(F32) + i1[...].astype(F32)).astype(BF16)
    for j in range(BACK_BLOCKS):
        out[:, j] = total[:, j * 128 : (j + 1) * 128].reshape(SRC, CAP, 128)


def unpack_back_kernel(got, gates, ids, slots, patch_grad, gate_grad, token):
    token[...] = jnp.zeros_like(token)
    m0, m1, _ = slot_match(ids[...], slots[...], CAP)
    sel = jnp.where(m0 | m1, 1.0, 0.0).astype(BF16)
    for j in range(SEND_BLOCKS):
        rows = got[:, j].reshape(ROWS, 128)
        patch_grad[:, pl.ds(j * 128, 128)] = dot_rows(sel, rows).astype(BF16)
    gate_block = got[:, SEND_BLOCKS].reshape(ROWS, 128)
    g = gates[...].astype(F32)
    for k, m in enumerate((m0, m1)):
        sel = jnp.where(m, 1.0, 0.0).astype(BF16)
        gate_grad[k : k + 1, :] = dot_rows(gate_block, sel)[0:1, :] / g[k : k + 1, :]


def shape(dims, kind=BF16):
    return jax.ShapeDtypeStruct(dims, kind)


ANY = pl.BlockSpec(memory_space=pl.ANY)
HBM = pl.BlockSpec(memory_space=pltpu.HBM)
VM = pl.BlockSpec(memory_space=pltpu.VMEM)


def call(kernel, out_shape, args, flops, moved, vmem, in_specs=None, out_specs=None, scratch=(), after=()):
    used = len(args)

    def body(*refs):
        kernel(*refs[:used], *refs[used + len(after) :])

    return pl.pallas_call(
        body,
        out_shape=out_shape,
        in_specs=(in_specs or [VM] * used) + [ANY] * len(after),
        out_specs=out_specs or jax.tree.map(lambda _: VM, out_shape),
        scratch_shapes=scratch,
        compiler_params=pltpu.CompilerParams(vmem_limit_bytes=vmem * 1024 * 1024),
        cost_estimate=pl.CostEstimate(flops=flops, bytes_accessed=moved, transcendentals=0),
    )(*args, *after)


def swap(value, axis, partner):
    return lax.ppermute(value, axis, [(i, partner(i)) for i in range(lax.axis_size(axis))])


def swap_rows(value):
    return swap(value, "x", lambda i: i ^ 1)


def swap_weights(value):
    return swap(value, "x", lambda i: 3 - i)


def swap_core(value):
    return swap(value, "core", lambda i: 1 - i)


def local(patches, upstream, gates, ids, slots, in_weights, out_weights):
    everywhere = ("zlo", "y", "zhi")
    gates, ids, slots = gates.T, ids.T, slots.T
    both = shape((2 * HS, D))
    wi00, wo00 = in_weights[0], out_weights[0]
    wi01, wo01 = swap_weights(wi00), swap_weights(wo00)
    wi10, wo10 = swap_core(wi00), swap_core(wo00)
    sent = call(
        pack_rows_kernel,
        shape((SRC, SEND_BLOCKS, 4, 128)),
        (gates, ids, slots, patches, upstream),
        500_000_000,
        5_000_000,
        60,
        in_specs=[HBM] * 5,
        out_specs=HBM,
        scratch=[
            pltpu.VMEM((2, T), BF16),
            pltpu.VMEM((2, T), I32),
            pltpu.VMEM((2, T), I32),
            pltpu.VMEM((T, D), BF16),
            pltpu.VMEM((T, D), BF16),
            pltpu.VMEM((SRC, SEND_BLOCKS, 4, 128), BF16),
            pltpu.SemaphoreType.DMA((5,)),
            pltpu.SemaphoreType.DMA((2,)),
        ],
    )
    got = lax.all_to_all(sent, everywhere, split_axis=0, concat_axis=0, tiled=True)
    own = call(
        unpack_rows_kernel,
        shape((2 * ROWS, D)),
        (got,),
        300_000_000,
        2_000_000,
        16,
        in_specs=[HBM],
        scratch=[
            pltpu.VMEM((SRC, SEND_BLOCKS, 4, 128), BF16),
            pltpu.VMEM((4 * SRC, D), BF16),
            pltpu.SemaphoreType.DMA((2,)),
        ],
    )
    other = swap_rows(own)
    wi11, wo11 = swap_core(wi01), swap_core(wo01)
    hidden = shape((4, ROWS, HS))
    turned = shape((D, 2 * PAD))

    def turn_call(*args):
        return call(turn_kernel, [turned, turned], args, 1_000_000, 5_000_000, 16)

    t_in0, t_out0 = turn_call(wi00, wi10, wo00, wo10)
    t_in1, t_out1 = turn_call(wi01, wi11, wo01, wo11)

    def expert_call(rows):
        return call(
            expert_kernel,
            [shape((ROWS, GW)), hidden, hidden],
            (rows, t_in0, t_in1, t_out0, t_out1, wi00, wi10, wi01, wi11),
            1_100_000_000,
            8_000_000,
            16,
        )

    part_own, pg_own, hid_own = expert_call(own)
    part_other, pg_other, hid_other = expert_call(other)
    part_back = swap_rows(part_other)
    saved = (own, other, pg_own, pg_other, hid_own, hid_other)

    def weight_call(c, add=(), after=()):
        return call(
            functools.partial(weight_kernel, c, len(add)),
            both,
            (*saved, *add),
            700_000_000,
            4_000_000,
            16,
            after=after,
        )

    far = weight_call(2, (swap_core(weight_call(3)),))
    sent = far
    far = swap_weights(far)
    near = swap_core(weight_call(1, after=(sent,)))
    mine = weight_call(0, after=(sent,))
    back = call(pack_back_kernel, shape((SRC, BACK_BLOCKS, CAP, 128)), (part_own, part_back), 300_000_000, 2_500_000, 16, after=(mine,))
    back = lax.all_to_all(back, everywhere, split_axis=0, concat_axis=0, tiled=True)
    patch_grad, gate_grad, token = call(
        unpack_back_kernel,
        [shape((T, D)), shape((2, T), F32), shape((8, 128), F32)],
        (back, gates, ids, slots),
        300_000_000,
        1_000_000,
        16,
    )
    mine = call(partial_sum_kernel, both, (mine, far), 1_000_000, 4_000_000, 16, after=(token,))
    grad_in, grad_out = call(
        weight_sum_kernel, [shape((HS, D))] * 2, (mine, near), 1_000_000, 4_000_000, 16, after=(token,)
    )
    return patch_grad, gate_grad.T, grad_in[None], grad_out[None]


def solution(mesh):
    names = ("zlo", "y", "x", "core", "zhi")
    split = Mesh(mesh.devices.reshape(4, 8, 4, 2, 2), names)
    tokens = P(names, None)
    weights = P(("zlo", "y"), ("x", "core", "zhi"), None)
    return jax.shard_map(
        local,
        mesh=split,
        in_specs=(tokens,) * 5 + (weights,) * 2,
        out_specs=(tokens, tokens, weights, weights),
        check_vma=False,
    )
```

```python
import functools

import jax
import jax.numpy as jnp
from jax import lax
from jax.experimental import pallas as pl
from jax.experimental.pallas import tpu as pltpu
from jax.sharding import Mesh, PartitionSpec as P

F32 = jnp.float32
BF16 = jnp.bfloat16
I32 = jnp.int32

CAP = 2
ROOT_TERM = 0.7978845608028654
CUBIC_TERM = 0.044715

T = 128
D = 1664
HS = 208
SRC = 64
ROWS = SRC * CAP
PAD = 256
GW = D + 128
SEND_BLOCKS = D // 128
BACK_BLOCKS = GW // 128


def dot(left, right):
    return jnp.dot(left, right, preferred_element_type=F32)


def dot_rows(left, right):
    return lax.dot_general(left, right, (((0,), (0,)), ((), ())), preferred_element_type=F32)


def dot_width(left, right):
    return lax.dot_general(left, right, (((1,), (1,)), ((), ())), preferred_element_type=F32)


def slot_match(ids, slots, per):
    target = jnp.where(slots >= 0, ids * CAP + slots, -1)
    row = lax.broadcasted_iota(I32, (SRC * per, T), 0)
    slot = row // (2 * per) * CAP + (row & 1)
    return target[0:1, :] == slot, target[1:2, :] == slot, row


def start_copies(pairs, sems):
    copies = [pltpu.make_async_copy(source, place, sems.at[k]) for k, (source, place) in enumerate(pairs)]
    for copy in copies:
        copy.start()
    return copies


def pack_rows_kernel(
    gates_in, ids_in, slots_in, patches_in, upstream_in, out,
    gates, ids, slots, patches, upstream, packed, sems, out_sems,
):
    copies = start_copies(
        [
            (ids_in, ids),
            (slots_in, slots),
            (gates_in, gates),
            (patches_in, patches),
            (upstream_in, upstream),
        ],
        sems,
    )
    for copy in copies[:3]:
        copy.wait()
    m0, m1, row = slot_match(ids[...], slots[...], 4)
    g = gates[...].astype(F32)
    gate = jnp.where(m0, g[0:1, :], 0.0) + jnp.where(m1, g[1:2, :], 0.0)
    is_up = (row & 2) != 0
    p_sel = jnp.where(is_up, 0.0, jnp.where(m0 | m1, 1.0, 0.0)).astype(BF16)
    u_sel = jnp.where(is_up, gate, 0.0).astype(BF16)
    for copy in copies[3:]:
        copy.wait()
    sent = []
    for half in range(2):
        part = SRC // 2
        rows = slice(half * part * 4, (half + 1) * part * 4)
        filled = (dot(p_sel[rows], patches[...]) + dot(u_sel[rows], upstream[...])).astype(BF16)
        place = pl.ds(half * part, part)
        for j in range(SEND_BLOCKS):
            packed[place, j] = filled[:, j * 128 : (j + 1) * 128].reshape(part, 4, 128)
        sent.append(pltpu.make_async_copy(packed.at[place], out.at[place], out_sems.at[half]))
        sent[-1].start()
    for copy in sent:
        copy.wait()


def unpack_rows_kernel(got, out, rows):
    o = lax.broadcasted_iota(I32, (2 * ROWS, 4 * SRC), 0)
    c = lax.broadcasted_iota(I32, (2 * ROWS, 4 * SRC), 1)
    want = ((o & (ROWS - 1)) >> 1) * 4 + o // ROWS * 2 + (o & 1)
    sel = jnp.where(c == want, 1.0, 0.0).astype(BF16)
    for j in range(SEND_BLOCKS):
        rows[:, pl.ds(j * 128, 128)] = got[:, j].reshape(4 * SRC, 128)
    out[...] = dot(sel, rows[...]).astype(BF16)


def gelu_and_slope(value):
    square = value * value
    tangent = jnp.tanh(ROOT_TERM * value * (1.0 + CUBIC_TERM * square))
    up = 0.5 * (1.0 + tangent)
    slope = up + 0.5 * value * (1.0 - tangent * tangent) * ROOT_TERM * (1.0 + 3.0 * CUBIC_TERM * square)
    return value * up, slope


def turn_kernel(in0, in1, out0, out1, in_turned, out_turned):
    for turned, parts in ((in_turned, (in0, in1)), (out_turned, (out0, out1))):
        for k, part in enumerate(parts):
            turned[:, pl.ds(k * PAD, HS)] = part[...].T
            turned[:, pl.ds(k * PAD + HS, PAD - HS)] = jnp.zeros((D, PAD - HS), BF16)


def expert_kernel(rows, t_in0, t_in1, t_out0, t_out1, w0, w1, w2, w3, part, pg_out, hid_out):
    p, u = rows[pl.ds(0, ROWS), :], rows[pl.ds(ROWS, ROWS), :]
    gate = jnp.zeros((ROWS, 1), F32)
    grads = []
    for c, (t_in, t_out) in enumerate(((t_in0, t_out0), (t_in1, t_out1))):
        pre = dot(p, t_in[...])
        back = dot(u, t_out[...])
        hid, slope = gelu_and_slope(pre)
        gate += jnp.sum(hid * back, axis=1, keepdims=True)
        pg = (back * slope).astype(BF16)
        hid = hid.astype(BF16)
        for k in range(2):
            own = slice(k * PAD, k * PAD + HS)
            pg_out[2 * c + k] = pg[:, own]
            hid_out[2 * c + k] = hid[:, own]
            grads.append(pg[:, own])
    total = sum(dot(grad, w[...]) for grad, w in zip(grads, (w0, w1, w2, w3)))
    part[:, :D] = total.astype(BF16)
    lane = lax.broadcasted_iota(I32, (ROWS, 128), 1)
    part[:, D:] = jnp.where(lane == 0, gate, 0.0).astype(BF16)


def weight_grads(c, rows0, rows1, pg0, pg1, hid0, hid1):
    p0, u0 = rows0[pl.ds(0, ROWS), :], rows0[pl.ds(ROWS, ROWS), :]
    p1, u1 = rows1[pl.ds(0, ROWS), :], rows1[pl.ds(ROWS, ROWS), :]
    return (
        dot_rows(pg0[c], p0) + dot_rows(pg1[c], p1),
        dot_rows(hid0[c], u0) + dot_rows(hid1[c], u1),
    )


def expert_and_far_kernel(*refs):
    rows, own, pg_own, hid_own = refs[0], *refs[9:12]
    part, pg_out, hid_out, far = refs[12:]
    expert_kernel(*refs[:9], part, pg_out, hid_out)
    weight_kernel(3, 0, own, rows, pg_own, pg_out, hid_own, hid_out, far)


def weight_kernel(c, add, *refs):
    out = refs[-1]
    grad_in, grad_out = weight_grads(c, *refs[:6])
    if add:
        got = refs[6]
        grad_in += got[pl.ds(0, HS), :].astype(F32)
        grad_out += got[pl.ds(HS, HS), :].astype(F32)
    out[pl.ds(0, HS), :] = grad_in.astype(BF16)
    out[pl.ds(HS, HS), :] = grad_out.astype(BF16)


def partial_sum_kernel(own, far, out):
    out[...] = (own[...].astype(F32) + far[...].astype(F32)).astype(BF16)


def weight_sum_kernel(own, near, out_in, out_out):
    for k, out in enumerate((out_in, out_out)):
        rows = pl.ds(k * HS, HS)
        out[...] = (own[rows, :].astype(F32) + near[rows, :].astype(F32)).astype(BF16)


def pack_back_kernel(i0, i1, out):
    total = (i0[...].astype(F32) + i1[...].astype(F32)).astype(BF16)
    for j in range(BACK_BLOCKS):
        out[:, j] = total[:, j * 128 : (j + 1) * 128].reshape(SRC, CAP, 128)


def unpack_back_kernel(got, gates, ids, slots, patch_grad, gate_grad, token):
    token[...] = jnp.zeros_like(token)
    m0, m1, _ = slot_match(ids[...], slots[...], CAP)
    sel = jnp.where(m0 | m1, 1.0, 0.0).astype(BF16)
    for j in range(SEND_BLOCKS):
        rows = got[:, j].reshape(ROWS, 128)
        patch_grad[:, pl.ds(j * 128, 128)] = dot_rows(sel, rows).astype(BF16)
    gate_block = got[:, SEND_BLOCKS].reshape(ROWS, 128)
    g = gates[...].astype(F32)
    for k, m in enumerate((m0, m1)):
        sel = jnp.where(m, 1.0, 0.0).astype(BF16)
        gate_grad[k : k + 1, :] = dot_rows(gate_block, sel)[0:1, :] / g[k : k + 1, :]


def shape(dims, kind=BF16):
    return jax.ShapeDtypeStruct(dims, kind)


ANY = pl.BlockSpec(memory_space=pl.ANY)
HBM = pl.BlockSpec(memory_space=pltpu.HBM)
VM = pl.BlockSpec(memory_space=pltpu.VMEM)


def call(kernel, out_shape, args, flops, moved, vmem, in_specs=None, out_specs=None, scratch=(), after=()):
    used = len(args)

    def body(*refs):
        kernel(*refs[:used], *refs[used + len(after) :])

    return pl.pallas_call(
        body,
        out_shape=out_shape,
        in_specs=(in_specs or [VM] * used) + [ANY] * len(after),
        out_specs=out_specs or jax.tree.map(lambda _: VM, out_shape),
        scratch_shapes=scratch,
        compiler_params=pltpu.CompilerParams(vmem_limit_bytes=vmem * 1024 * 1024),
        cost_estimate=pl.CostEstimate(flops=flops, bytes_accessed=moved, transcendentals=0),
    )(*args, *after)


def swap(value, axis, partner):
    return lax.ppermute(value, axis, [(i, partner(i)) for i in range(lax.axis_size(axis))])


def swap_rows(value):
    return swap(value, "x", lambda i: i ^ 1)


def swap_weights(value):
    return swap(value, "x", lambda i: 3 - i)


def swap_core(value):
    return swap(value, "core", lambda i: 1 - i)


def local(patches, upstream, gates, ids, slots, in_weights, out_weights):
    everywhere = ("zlo", "y", "zhi")
    gates, ids, slots = gates.T, ids.T, slots.T
    both = shape((2 * HS, D))
    wi00, wo00 = in_weights[0], out_weights[0]
    wi01, wo01 = swap_weights(wi00), swap_weights(wo00)
    wi10, wo10 = swap_core(wi00), swap_core(wo00)
    sent = call(
        pack_rows_kernel,
        shape((SRC, SEND_BLOCKS, 4, 128)),
        (gates, ids, slots, patches, upstream),
        500_000_000,
        5_000_000,
        60,
        in_specs=[HBM] * 5,
        out_specs=HBM,
        scratch=[
            pltpu.VMEM((2, T), BF16),
            pltpu.VMEM((2, T), I32),
            pltpu.VMEM((2, T), I32),
            pltpu.VMEM((T, D), BF16),
            pltpu.VMEM((T, D), BF16),
            pltpu.VMEM((SRC, SEND_BLOCKS, 4, 128), BF16),
            pltpu.SemaphoreType.DMA((5,)),
            pltpu.SemaphoreType.DMA((2,)),
        ],
    )
    got = lax.all_to_all(sent, everywhere, split_axis=0, concat_axis=0, tiled=True)
    own = call(
        unpack_rows_kernel,
        shape((2 * ROWS, D)),
        (got,),
        300_000_000,
        2_000_000,
        16,
        scratch=[pltpu.VMEM((4 * SRC, D), BF16)],
    )
    other = swap_rows(own)
    wi11, wo11 = swap_core(wi01), swap_core(wo01)
    hidden = shape((4, ROWS, HS))
    turned = shape((D, 2 * PAD))

    def turn_call(*args):
        return call(turn_kernel, [turned, turned], args, 1_000_000, 5_000_000, 16)

    t_in0, t_out0 = turn_call(wi00, wi10, wo00, wo10)
    t_in1, t_out1 = turn_call(wi01, wi11, wo01, wo11)

    weights = (t_in0, t_in1, t_out0, t_out1, wi00, wi10, wi01, wi11)
    part_own, pg_own, hid_own = call(
        expert_kernel, [shape((ROWS, GW)), hidden, hidden], (own, *weights), 1_100_000_000, 8_000_000, 16
    )
    part_other, pg_other, hid_other, far = call(
        expert_and_far_kernel,
        [shape((ROWS, GW)), hidden, hidden, both],
        (other, *weights, own, pg_own, hid_own),
        1_500_000_000,
        10_000_000,
        16,
    )
    part_back = swap_rows(part_other)
    saved = (own, other, pg_own, pg_other, hid_own, hid_other)

    def weight_call(c, add=(), after=()):
        return call(
            functools.partial(weight_kernel, c, len(add)),
            both,
            (*saved, *add),
            700_000_000,
            4_000_000,
            16,
            after=after,
        )

    far = weight_call(2, (swap_core(far),))
    sent = far
    far = swap_weights(far)
    near = swap_core(weight_call(1, after=(sent,)))
    mine = weight_call(0, after=(sent,))
    back = call(
        pack_back_kernel,
        shape((SRC, BACK_BLOCKS, CAP, 128)),
        (part_own, part_back),
        300_000_000,
        2_500_000,
        16,
        after=(mine,),
    )
    back = lax.all_to_all(back, everywhere, split_axis=0, concat_axis=0, tiled=True)
    patch_grad, gate_grad, token = call(
        unpack_back_kernel,
        [shape((T, D)), shape((2, T), F32), shape((8, 128), F32)],
        (back, gates, ids, slots),
        300_000_000,
        1_000_000,
        16,
    )
    mine = call(partial_sum_kernel, both, (mine, far), 1_000_000, 4_000_000, 16, after=(token,))
    grad_in, grad_out = call(
        weight_sum_kernel, [shape((HS, D))] * 2, (mine, near), 1_000_000, 4_000_000, 16, after=(token,)
    )
    return patch_grad, gate_grad.T, grad_in[None], grad_out[None]


def solution(mesh):
    names = ("zlo", "y", "x", "core", "zhi")
    split = Mesh(mesh.devices.reshape(4, 8, 4, 2, 2), names)
    tokens = P(names, None)
    weights = P(("zlo", "y"), ("x", "core", "zhi"), None)
    return jax.shard_map(
        local,
        mesh=split,
        in_specs=(tokens,) * 5 + (weights,) * 2,
        out_specs=(tokens, tokens, weights, weights),
        check_vma=False,
    )
```

```python
import functools

import jax
import jax.numpy as jnp
from jax import lax
from jax.experimental import pallas as pl
from jax.experimental.pallas import tpu as pltpu
from jax.sharding import Mesh, PartitionSpec as P

F32 = jnp.float32
BF16 = jnp.bfloat16
I32 = jnp.int32

CAP = 2
ROOT_TERM = 0.7978845608028654
CUBIC_TERM = 0.044715

T = 128
D = 1664
HS = 208
SRC = 64
ROWS = SRC * CAP
PAD = 256
GW = D + 128
SEND_BLOCKS = D // 128
BACK_BLOCKS = GW // 128


def dot(left, right):
    return jnp.dot(left, right, preferred_element_type=F32)


def dot_rows(left, right):
    return lax.dot_general(left, right, (((0,), (0,)), ((), ())), preferred_element_type=F32)


def dot_width(left, right):
    return lax.dot_general(left, right, (((1,), (1,)), ((), ())), preferred_element_type=F32)


def slot_match(ids, slots, per):
    target = jnp.where(slots >= 0, ids * CAP + slots, -1)
    row = lax.broadcasted_iota(I32, (SRC * per, T), 0)
    slot = row // (2 * per) * CAP + (row & 1)
    return target[0:1, :] == slot, target[1:2, :] == slot, row


def start_copies(pairs, sems):
    copies = [pltpu.make_async_copy(source, place, sems.at[k]) for k, (source, place) in enumerate(pairs)]
    for copy in copies:
        copy.start()
    return copies


def pack_rows_kernel(
    gates_in, ids_in, slots_in, patches_in, upstream_in, out,
    gates, ids, slots, patches, upstream, packed, sems, out_sems,
):
    copies = start_copies(
        [
            (ids_in, ids),
            (slots_in, slots),
            (gates_in, gates),
            (patches_in, patches),
            (upstream_in, upstream),
        ],
        sems,
    )
    for copy in copies[:3]:
        copy.wait()
    m0, m1, row = slot_match(ids[...], slots[...], 4)
    g = gates[...].astype(F32)
    gate = jnp.where(m0, g[0:1, :], 0.0) + jnp.where(m1, g[1:2, :], 0.0)
    is_up = (row & 2) != 0
    p_sel = jnp.where(is_up, 0.0, jnp.where(m0 | m1, 1.0, 0.0)).astype(BF16)
    u_sel = jnp.where(is_up, gate, 0.0).astype(BF16)
    for copy in copies[3:]:
        copy.wait()
    sent = []
    for half in range(2):
        part = SRC // 2
        rows = slice(half * part * 4, (half + 1) * part * 4)
        filled = (dot(p_sel[rows], patches[...]) + dot(u_sel[rows], upstream[...])).astype(BF16)
        place = pl.ds(half * part, part)
        for j in range(SEND_BLOCKS):
            packed[place, j] = filled[:, j * 128 : (j + 1) * 128].reshape(part, 4, 128)
        sent.append(pltpu.make_async_copy(packed.at[place], out.at[place], out_sems.at[half]))
        sent[-1].start()
    for copy in sent:
        copy.wait()


def unpack_rows_kernel(got, out, rows):
    o = lax.broadcasted_iota(I32, (2 * ROWS, 4 * SRC), 0)
    c = lax.broadcasted_iota(I32, (2 * ROWS, 4 * SRC), 1)
    want = ((o & (ROWS - 1)) >> 1) * 4 + o // ROWS * 2 + (o & 1)
    sel = jnp.where(c == want, 1.0, 0.0).astype(BF16)
    for j in range(SEND_BLOCKS):
        rows[:, pl.ds(j * 128, 128)] = got[:, j].reshape(4 * SRC, 128)
    out[...] = dot(sel, rows[...]).astype(BF16)


def gelu_and_slope(value):
    square = value * value
    tangent = jnp.tanh(ROOT_TERM * value * (1.0 + CUBIC_TERM * square))
    up = 0.5 * (1.0 + tangent)
    slope = up + 0.5 * value * (1.0 - tangent * tangent) * ROOT_TERM * (1.0 + 3.0 * CUBIC_TERM * square)
    return value * up, slope


def turn_kernel(in0, in1, out0, out1, in_turned, out_turned):
    for turned, parts in ((in_turned, (in0, in1)), (out_turned, (out0, out1))):
        for k, part in enumerate(parts):
            turned[:, pl.ds(k * PAD, HS)] = part[...].T
            turned[:, pl.ds(k * PAD + HS, PAD - HS)] = jnp.zeros((D, PAD - HS), BF16)


def expert_kernel(rows, t_in0, t_in1, t_out0, t_out1, w0, w1, w2, w3, part, pg_out, hid_out):
    p, u = rows[pl.ds(0, ROWS), :], rows[pl.ds(ROWS, ROWS), :]
    gate = jnp.zeros((ROWS, 1), F32)
    grads = []
    for c, (t_in, t_out) in enumerate(((t_in0, t_out0), (t_in1, t_out1))):
        pre = dot(p, t_in[...])
        back = dot(u, t_out[...])
        hid, slope = gelu_and_slope(pre)
        gate += jnp.sum(hid * back, axis=1, keepdims=True)
        pg = (back * slope).astype(BF16)
        hid = hid.astype(BF16)
        for k in range(2):
            own = slice(k * PAD, k * PAD + HS)
            pg_out[2 * c + k] = pg[:, own]
            hid_out[2 * c + k] = hid[:, own]
            grads.append(pg[:, own])
    total = sum(dot(grad, w[...]) for grad, w in zip(grads, (w0, w1, w2, w3)))
    part[:, :D] = total.astype(BF16)
    lane = lax.broadcasted_iota(I32, (ROWS, 128), 1)
    part[:, D:] = jnp.where(lane == 0, gate, 0.0).astype(BF16)


def weight_grads(c, rows0, rows1, pg0, pg1, hid0, hid1):
    p0, u0 = rows0[pl.ds(0, ROWS), :], rows0[pl.ds(ROWS, ROWS), :]
    p1, u1 = rows1[pl.ds(0, ROWS), :], rows1[pl.ds(ROWS, ROWS), :]
    return (
        dot_rows(pg0[c], p0) + dot_rows(pg1[c], p1),
        dot_rows(hid0[c], u0) + dot_rows(hid1[c], u1),
    )


def expert_and_far_kernel(*refs):
    rows, own, pg_own, hid_own = refs[0], *refs[9:12]
    part, pg_out, hid_out, far = refs[12:]
    expert_kernel(*refs[:9], part, pg_out, hid_out)
    weight_kernel(3, 0, own, rows, pg_own, pg_out, hid_own, hid_out, far)


def weight_kernel(c, add, *refs):
    out = refs[-1]
    grad_in, grad_out = weight_grads(c, *refs[:6])
    if add:
        got = refs[6]
        grad_in += got[pl.ds(0, HS), :].astype(F32)
        grad_out += got[pl.ds(HS, HS), :].astype(F32)
    out[pl.ds(0, HS), :] = grad_in.astype(BF16)
    out[pl.ds(HS, HS), :] = grad_out.astype(BF16)


def partial_sum_kernel(own, far, out):
    out[...] = (own[...].astype(F32) + far[...].astype(F32)).astype(BF16)


def pack_back_kernel(i0, i1, out):
    total = (i0[...].astype(F32) + i1[...].astype(F32)).astype(BF16)
    for j in range(BACK_BLOCKS):
        out[:, j] = total[:, j * 128 : (j + 1) * 128].reshape(SRC, CAP, 128)


def mask_kernel(gates, ids, slots, masks, wide_gates):
    m0, m1, _ = slot_match(ids[...], slots[...], CAP)
    for k, m in enumerate((m0, m1, m0 | m1)):
        masks[k] = jnp.where(m, 1.0, 0.0).astype(BF16)
    wide_gates[...] = gates[...].astype(F32)


def last_kernel(got, masks, wide_gates, own, near, patch_grad, gate_grad, out_in, out_out, sums, rows, sems):
    sums[...] = (own[...].astype(F32) + near[...].astype(F32)).astype(BF16)
    copies = start_copies([(sums.at[pl.ds(0, HS), :], out_in), (sums.at[pl.ds(HS, HS), :], out_out)], sems)
    for j in range(SEND_BLOCKS):
        rows[:, pl.ds(j * 128, 128)] = got[:, j].reshape(ROWS, 128)
    patch_grad[...] = dot_rows(masks[2], rows[...]).astype(BF16)
    gate_block = got[:, SEND_BLOCKS].reshape(ROWS, 128)
    for k in range(2):
        gate_grad[k : k + 1, :] = dot_rows(gate_block, masks[k])[0:1, :] / wide_gates[k : k + 1, :]
    for copy in copies:
        copy.wait()


def shape(dims, kind=BF16):
    return jax.ShapeDtypeStruct(dims, kind)


ANY = pl.BlockSpec(memory_space=pl.ANY)
HBM = pl.BlockSpec(memory_space=pltpu.HBM)
VM = pl.BlockSpec(memory_space=pltpu.VMEM)


def call(kernel, out_shape, args, flops, moved, vmem, in_specs=None, out_specs=None, scratch=(), after=()):
    used = len(args)

    def body(*refs):
        kernel(*refs[:used], *refs[used + len(after) :])

    return pl.pallas_call(
        body,
        out_shape=out_shape,
        in_specs=(in_specs or [VM] * used) + [ANY] * len(after),
        out_specs=out_specs or jax.tree.map(lambda _: VM, out_shape),
        scratch_shapes=scratch,
        compiler_params=pltpu.CompilerParams(vmem_limit_bytes=vmem * 1024 * 1024),
        cost_estimate=pl.CostEstimate(flops=flops, bytes_accessed=moved, transcendentals=0),
    )(*args, *after)


def swap(value, axis, partner):
    return lax.ppermute(value, axis, [(i, partner(i)) for i in range(lax.axis_size(axis))])


def swap_rows(value):
    return swap(value, "x", lambda i: i ^ 1)


def swap_weights(value):
    return swap(value, "x", lambda i: 3 - i)


def swap_core(value):
    return swap(value, "core", lambda i: 1 - i)


def local(patches, upstream, gates, ids, slots, in_weights, out_weights):
    everywhere = ("zlo", "y", "zhi")
    gates, ids, slots = gates.T, ids.T, slots.T
    both = shape((2 * HS, D))
    wi00, wo00 = in_weights[0], out_weights[0]
    wi01, wo01 = swap_weights(wi00), swap_weights(wo00)
    wi10, wo10 = swap_core(wi00), swap_core(wo00)
    sent = call(
        pack_rows_kernel,
        shape((SRC, SEND_BLOCKS, 4, 128)),
        (gates, ids, slots, patches, upstream),
        500_000_000,
        5_000_000,
        60,
        in_specs=[HBM] * 5,
        out_specs=HBM,
        scratch=[
            pltpu.VMEM((2, T), BF16),
            pltpu.VMEM((2, T), I32),
            pltpu.VMEM((2, T), I32),
            pltpu.VMEM((T, D), BF16),
            pltpu.VMEM((T, D), BF16),
            pltpu.VMEM((SRC, SEND_BLOCKS, 4, 128), BF16),
            pltpu.SemaphoreType.DMA((5,)),
            pltpu.SemaphoreType.DMA((2,)),
        ],
    )
    got = lax.all_to_all(sent, everywhere, split_axis=0, concat_axis=0, tiled=True)
    own = call(
        unpack_rows_kernel,
        shape((2 * ROWS, D)),
        (got,),
        300_000_000,
        2_000_000,
        16,
        scratch=[pltpu.VMEM((4 * SRC, D), BF16)],
    )
    other = swap_rows(own)
    wi11, wo11 = swap_core(wi01), swap_core(wo01)
    hidden = shape((4, ROWS, HS))
    turned = shape((D, 2 * PAD))

    def turn_call(*args):
        return call(turn_kernel, [turned, turned], args, 1_000_000, 5_000_000, 16)

    t_in0, t_out0 = turn_call(wi00, wi10, wo00, wo10)
    t_in1, t_out1 = turn_call(wi01, wi11, wo01, wo11)

    weights = (t_in0, t_in1, t_out0, t_out1, wi00, wi10, wi01, wi11)
    part_own, pg_own, hid_own = call(
        expert_kernel, [shape((ROWS, GW)), hidden, hidden], (own, *weights), 1_100_000_000, 8_000_000, 16
    )
    part_other, pg_other, hid_other, far = call(
        expert_and_far_kernel,
        [shape((ROWS, GW)), hidden, hidden, both],
        (other, *weights, own, pg_own, hid_own),
        1_500_000_000,
        10_000_000,
        16,
    )
    part_back = swap_rows(part_other)
    saved = (own, other, pg_own, pg_other, hid_own, hid_other)

    def weight_call(c, add=(), after=()):
        return call(
            functools.partial(weight_kernel, c, len(add)),
            both,
            (*saved, *add),
            700_000_000,
            4_000_000,
            16,
            after=after,
        )

    far = weight_call(2, (swap_core(far),))
    sent = far
    far = swap_weights(far)
    near = swap_core(weight_call(1, after=(sent,)))
    mine = weight_call(0, after=(sent,))
    masks, wide_gates = call(
        mask_kernel,
        [shape((3, ROWS, T)), shape((2, T), F32)],
        (gates, ids, slots),
        1_000_000,
        100_000,
        16,
        after=(sent,),
    )
    back = call(
        pack_back_kernel,
        shape((SRC, BACK_BLOCKS, CAP, 128)),
        (part_own, part_back),
        300_000_000,
        2_500_000,
        16,
        after=(mine, masks),
    )
    back = lax.all_to_all(back, everywhere, split_axis=0, concat_axis=0, tiled=True)
    mine = call(partial_sum_kernel, both, (mine, far), 1_000_000, 4_000_000, 16, after=(back,))
    patch_grad, gate_grad, grad_in, grad_out = call(
        last_kernel,
        [shape((T, D)), shape((2, T), F32), shape((HS, D)), shape((HS, D))],
        (back, masks, wide_gates, mine, near),
        300_000_000,
        6_000_000,
        16,
        out_specs=[VM, VM, HBM, HBM],
        scratch=[pltpu.VMEM((2 * HS, D), BF16), pltpu.VMEM((ROWS, D), BF16), pltpu.SemaphoreType.DMA((2,))],
    )
    return patch_grad, gate_grad.T, grad_in[None], grad_out[None]


def solution(mesh):
    names = ("zlo", "y", "x", "core", "zhi")
    split = Mesh(mesh.devices.reshape(4, 8, 4, 2, 2), names)
    tokens = P(names, None)
    weights = P(("zlo", "y"), ("x", "core", "zhi"), None)
    return jax.shard_map(
        local,
        mesh=split,
        in_specs=(tokens,) * 5 + (weights,) * 2,
        out_specs=(tokens, tokens, weights, weights),
        check_vma=False,
    )
```

```python
import functools

import jax
import jax.numpy as jnp
from jax import lax
from jax.experimental import pallas as pl
from jax.experimental.pallas import tpu as pltpu
from jax.sharding import Mesh, PartitionSpec as P

F32 = jnp.float32
BF16 = jnp.bfloat16
I32 = jnp.int32

CAP = 2
ROOT_TERM = 0.7978845608028654
CUBIC_TERM = 0.044715

T = 128
D = 1664
HS = 208
SRC = 64
ROWS = SRC * CAP
PAD = 256
GW = D + 128
SEND_BLOCKS = D // 128
BACK_BLOCKS = GW // 128


def dot(left, right):
    return jnp.dot(left, right, preferred_element_type=F32)


def dot_rows(left, right):
    return lax.dot_general(left, right, (((0,), (0,)), ((), ())), preferred_element_type=F32)


def dot_width(left, right):
    return lax.dot_general(left, right, (((1,), (1,)), ((), ())), preferred_element_type=F32)


def slot_match(ids, slots, per):
    target = jnp.where(slots >= 0, ids * CAP + slots, -1)
    row = lax.broadcasted_iota(I32, (SRC * per, T), 0)
    slot = row // (2 * per) * CAP + (row & 1)
    return target[0:1, :] == slot, target[1:2, :] == slot, row


def start_copies(pairs, sems):
    copies = [pltpu.make_async_copy(source, place, sems.at[k]) for k, (source, place) in enumerate(pairs)]
    for copy in copies:
        copy.start()
    return copies


def pack_rows_kernel(
    gates_in, ids_in, slots_in, patches_in, upstream_in, out,
    gates, ids, slots, patches, upstream, packed, sems, out_sems,
):
    copies = start_copies(
        [
            (ids_in, ids),
            (slots_in, slots),
            (gates_in, gates),
            (patches_in, patches),
            (upstream_in, upstream),
        ],
        sems,
    )
    for copy in copies[:3]:
        copy.wait()
    m0, m1, row = slot_match(ids[...], slots[...], 4)
    g = gates[...].astype(F32)
    gate = jnp.where(m0, g[0:1, :], 0.0) + jnp.where(m1, g[1:2, :], 0.0)
    is_up = (row & 2) != 0
    p_sel = jnp.where(is_up, 0.0, jnp.where(m0 | m1, 1.0, 0.0)).astype(BF16)
    u_sel = jnp.where(is_up, gate, 0.0).astype(BF16)
    for copy in copies[3:]:
        copy.wait()
    sent = []
    for half in range(2):
        part = SRC // 2
        rows = slice(half * part * 4, (half + 1) * part * 4)
        filled = (dot(p_sel[rows], patches[...]) + dot(u_sel[rows], upstream[...])).astype(BF16)
        place = pl.ds(half * part, part)
        for j in range(SEND_BLOCKS):
            packed[place, j] = filled[:, j * 128 : (j + 1) * 128].reshape(part, 4, 128)
        sent.append(pltpu.make_async_copy(packed.at[place], out.at[place], out_sems.at[half]))
        sent[-1].start()
    for copy in sent:
        copy.wait()


def unpack_rows_kernel(got, out, rows):
    o = lax.broadcasted_iota(I32, (2 * ROWS, 4 * SRC), 0)
    c = lax.broadcasted_iota(I32, (2 * ROWS, 4 * SRC), 1)
    want = ((o & (ROWS - 1)) >> 1) * 4 + o // ROWS * 2 + (o & 1)
    sel = jnp.where(c == want, 1.0, 0.0).astype(BF16)
    for j in range(SEND_BLOCKS):
        rows[:, pl.ds(j * 128, 128)] = got[:, j].reshape(4 * SRC, 128)
    out[...] = dot(sel, rows[...]).astype(BF16)


def gelu_and_slope(value):
    square = value * value
    tangent = jnp.tanh(ROOT_TERM * value * (1.0 + CUBIC_TERM * square))
    up = 0.5 * (1.0 + tangent)
    slope = up + 0.5 * value * (1.0 - tangent * tangent) * ROOT_TERM * (1.0 + 3.0 * CUBIC_TERM * square)
    return value * up, slope


def turn_kernel(in0, in1, out0, out1, in_turned, out_turned):
    for turned, parts in ((in_turned, (in0, in1)), (out_turned, (out0, out1))):
        for k, part in enumerate(parts):
            turned[:, pl.ds(k * PAD, HS)] = part[...].T
            turned[:, pl.ds(k * PAD + HS, PAD - HS)] = jnp.zeros((D, PAD - HS), BF16)


def expert_kernel(rows, t_in0, t_in1, t_out0, t_out1, w0, w1, w2, w3, part, pg_out, hid_out):
    p, u = rows[pl.ds(0, ROWS), :], rows[pl.ds(ROWS, ROWS), :]
    gate = jnp.zeros((ROWS, 1), F32)
    grads = []
    for c, (t_in, t_out) in enumerate(((t_in0, t_out0), (t_in1, t_out1))):
        pre = dot(p, t_in[...])
        back = dot(u, t_out[...])
        hid, slope = gelu_and_slope(pre)
        gate += jnp.sum(hid * back, axis=1, keepdims=True)
        pg = (back * slope).astype(BF16)
        hid = hid.astype(BF16)
        for k in range(2):
            own = slice(k * PAD, k * PAD + HS)
            pg_out[2 * c + k] = pg[:, own]
            hid_out[2 * c + k] = hid[:, own]
            grads.append(pg[:, own])
    total = sum(dot(grad, w[...]) for grad, w in zip(grads, (w0, w1, w2, w3)))
    part[:, :D] = total.astype(BF16)
    lane = lax.broadcasted_iota(I32, (ROWS, 128), 1)
    part[:, D:] = jnp.where(lane == 0, gate, 0.0).astype(BF16)


def weight_grads(c, rows0, rows1, pg0, pg1, hid0, hid1):
    p0, u0 = rows0[pl.ds(0, ROWS), :], rows0[pl.ds(ROWS, ROWS), :]
    p1, u1 = rows1[pl.ds(0, ROWS), :], rows1[pl.ds(ROWS, ROWS), :]
    return (
        dot_rows(pg0[c], p0) + dot_rows(pg1[c], p1),
        dot_rows(hid0[c], u0) + dot_rows(hid1[c], u1),
    )


def expert_and_far_kernel(*refs):
    rows, own, pg_own, hid_own = refs[0], *refs[9:12]
    part, pg_out, hid_out, far = refs[12:]
    expert_kernel(*refs[:9], part, pg_out, hid_out)
    weight_kernel(3, 0, own, rows, pg_own, pg_out, hid_own, hid_out, far)


def weight_kernel(c, add, *refs):
    out = refs[-1]
    grad_in, grad_out = weight_grads(c, *refs[:6])
    if add:
        got = refs[6]
        grad_in += got[pl.ds(0, HS), :].astype(F32)
        grad_out += got[pl.ds(HS, HS), :].astype(F32)
    out[pl.ds(0, HS), :] = grad_in.astype(BF16)
    out[pl.ds(HS, HS), :] = grad_out.astype(BF16)


def partial_sum_kernel(own, far, out):
    out[...] = (own[...].astype(F32) + far[...].astype(F32)).astype(BF16)


def weight_sum_kernel(own, near, out_in, out_out, sums, sems):
    copies = []
    for k, out in enumerate((out_in, out_out)):
        rows = pl.ds(k * HS, HS)
        sums[rows, :] = (own[rows, :].astype(F32) + near[rows, :].astype(F32)).astype(BF16)
        copies.append(pltpu.make_async_copy(sums.at[rows, :], out, sems.at[k]))
        copies[-1].start()
    for copy in copies:
        copy.wait()


def pack_back_kernel(i0, i1, out):
    total = (i0[...].astype(F32) + i1[...].astype(F32)).astype(BF16)
    for j in range(BACK_BLOCKS):
        out[:, j] = total[:, j * 128 : (j + 1) * 128].reshape(SRC, CAP, 128)


def mask_kernel(gates, ids, slots, masks, wide_gates):
    m0, m1, _ = slot_match(ids[...], slots[...], CAP)
    for k, m in enumerate((m0, m1, m0 | m1)):
        masks[k] = jnp.where(m, 1.0, 0.0).astype(BF16)
    wide_gates[...] = gates[...].astype(F32)


def unpack_back_kernel(got, masks, wide_gates, patch_grad, gate_grad, token):
    token[...] = jnp.zeros_like(token)
    for j in range(SEND_BLOCKS):
        rows = got[:, j].reshape(ROWS, 128)
        patch_grad[:, pl.ds(j * 128, 128)] = dot_rows(masks[2], rows).astype(BF16)
    gate_block = got[:, SEND_BLOCKS].reshape(ROWS, 128)
    for k in range(2):
        gate_grad[k : k + 1, :] = dot_rows(gate_block, masks[k])[0:1, :] / wide_gates[k : k + 1, :]


def shape(dims, kind=BF16):
    return jax.ShapeDtypeStruct(dims, kind)


ANY = pl.BlockSpec(memory_space=pl.ANY)
HBM = pl.BlockSpec(memory_space=pltpu.HBM)
VM = pl.BlockSpec(memory_space=pltpu.VMEM)


def call(kernel, out_shape, args, flops, moved, vmem, in_specs=None, out_specs=None, scratch=(), after=()):
    used = len(args)

    def body(*refs):
        kernel(*refs[:used], *refs[used + len(after) :])

    return pl.pallas_call(
        body,
        out_shape=out_shape,
        in_specs=(in_specs or [VM] * used) + [ANY] * len(after),
        out_specs=out_specs or jax.tree.map(lambda _: VM, out_shape),
        scratch_shapes=scratch,
        compiler_params=pltpu.CompilerParams(vmem_limit_bytes=vmem * 1024 * 1024),
        cost_estimate=pl.CostEstimate(flops=flops, bytes_accessed=moved, transcendentals=0),
    )(*args, *after)


def swap(value, axis, partner):
    return lax.ppermute(value, axis, [(i, partner(i)) for i in range(lax.axis_size(axis))])


def swap_rows(value):
    return swap(value, "x", lambda i: i ^ 1)


def swap_weights(value):
    return swap(value, "x", lambda i: 3 - i)


def swap_core(value):
    return swap(value, "core", lambda i: 1 - i)


def local(patches, upstream, gates, ids, slots, in_weights, out_weights):
    everywhere = ("zlo", "y", "zhi")
    gates, ids, slots = gates.T, ids.T, slots.T
    both = shape((2 * HS, D))
    wi00, wo00 = in_weights[0], out_weights[0]
    wi01, wo01 = swap_weights(wi00), swap_weights(wo00)
    wi10, wo10 = swap_core(wi00), swap_core(wo00)
    sent = call(
        pack_rows_kernel,
        shape((SRC, SEND_BLOCKS, 4, 128)),
        (gates, ids, slots, patches, upstream),
        500_000_000,
        5_000_000,
        60,
        in_specs=[HBM] * 5,
        out_specs=HBM,
        scratch=[
            pltpu.VMEM((2, T), BF16),
            pltpu.VMEM((2, T), I32),
            pltpu.VMEM((2, T), I32),
            pltpu.VMEM((T, D), BF16),
            pltpu.VMEM((T, D), BF16),
            pltpu.VMEM((SRC, SEND_BLOCKS, 4, 128), BF16),
            pltpu.SemaphoreType.DMA((5,)),
            pltpu.SemaphoreType.DMA((2,)),
        ],
    )
    got = lax.all_to_all(sent, everywhere, split_axis=0, concat_axis=0, tiled=True)
    own = call(
        unpack_rows_kernel,
        shape((2 * ROWS, D)),
        (got,),
        300_000_000,
        2_000_000,
        16,
        scratch=[pltpu.VMEM((4 * SRC, D), BF16)],
    )
    other = swap_rows(own)
    wi11, wo11 = swap_core(wi01), swap_core(wo01)
    hidden = shape((4, ROWS, HS))
    turned = shape((D, 2 * PAD))

    def turn_call(*args):
        return call(turn_kernel, [turned, turned], args, 1_000_000, 5_000_000, 16)

    t_in0, t_out0 = turn_call(wi00, wi10, wo00, wo10)
    t_in1, t_out1 = turn_call(wi01, wi11, wo01, wo11)

    weights = (t_in0, t_in1, t_out0, t_out1, wi00, wi10, wi01, wi11)
    part_own, pg_own, hid_own = call(
        expert_kernel, [shape((ROWS, GW)), hidden, hidden], (own, *weights), 1_100_000_000, 8_000_000, 16
    )
    part_other, pg_other, hid_other, far = call(
        expert_and_far_kernel,
        [shape((ROWS, GW)), hidden, hidden, both],
        (other, *weights, own, pg_own, hid_own),
        1_500_000_000,
        10_000_000,
        16,
    )
    part_back = swap_rows(part_other)
    saved = (own, other, pg_own, pg_other, hid_own, hid_other)

    def weight_call(c, add=(), after=()):
        return call(
            functools.partial(weight_kernel, c, len(add)),
            both,
            (*saved, *add),
            700_000_000,
            4_000_000,
            16,
            after=after,
        )

    far = weight_call(2, (swap_core(far),))
    sent = far
    far = swap_weights(far)
    near = swap_core(weight_call(1, after=(sent,)))
    mine = weight_call(0, after=(sent,))
    masks, wide_gates = call(
        mask_kernel,
        [shape((3, ROWS, T)), shape((2, T), F32)],
        (gates, ids, slots),
        1_000_000,
        100_000,
        16,
        after=(sent,),
    )
    back = call(
        pack_back_kernel,
        shape((SRC, BACK_BLOCKS, CAP, 128)),
        (part_own, part_back),
        300_000_000,
        2_500_000,
        16,
        after=(mine, masks),
    )
    back = lax.all_to_all(back, everywhere, split_axis=0, concat_axis=0, tiled=True)
    patch_grad, gate_grad, token = call(
        unpack_back_kernel,
        [shape((T, D)), shape((2, T), F32), shape((8, 128), F32)],
        (back, masks, wide_gates),
        300_000_000,
        1_000_000,
        16,
    )
    mine = call(partial_sum_kernel, both, (mine, far), 1_000_000, 4_000_000, 16, after=(token,))
    grad_in, grad_out = call(
        weight_sum_kernel,
        [shape((HS, D))] * 2,
        (mine, near),
        1_000_000,
        4_000_000,
        16,
        out_specs=[HBM] * 2,
        scratch=[pltpu.VMEM((2 * HS, D), BF16), pltpu.SemaphoreType.DMA((2,))],
        after=(token,),
    )
    return patch_grad, gate_grad.T, grad_in[None], grad_out[None]


def solution(mesh):
    names = ("zlo", "y", "x", "core", "zhi")
    split = Mesh(mesh.devices.reshape(4, 8, 4, 2, 2), names)
    tokens = P(names, None)
    weights = P(("zlo", "y"), ("x", "core", "zhi"), None)
    return jax.shard_map(
        local,
        mesh=split,
        in_specs=(tokens,) * 5 + (weights,) * 2,
        out_specs=(tokens, tokens, weights, weights),
        check_vma=False,
    )
```
